32 devices in a mesh: sec: 2 (over x), blk: 16 (over z, y, core).
Axes of the slice: x: 2, y: 2, z: 4, core: 2. Of those that a mesh axis runs over, the one named last changes fastest.
Arguments:
- column_state: float32 [2, 64, 512, 512], P('sec', None, 'blk'), may hold values from -6 to 6
- forcing: bfloat16 [2, 8, 512, 512], P('sec', None, 'blk'), may hold values from -6 to 6
- couple_gain: bfloat16 [2, 64, 8], P('sec'), may hold values from -2 to 2
- diffusion: float32 [2, 64], P('sec'), may hold values from 0.2 to 0.24
- mixing: float32 [2, 64, 64], P('sec'), may hold values from -0.75 to 0.75
- export_map: float32 [2, 8, 64], P('sec'), may hold values from -0.75 to 0.75
- land_mask: int32 [512, 512], P('blk'), may hold values 0 or 1
- sources: int32 [2, 2048, 3], P('sec', 'blk'), may hold values from 0 to 2047, as said below
- regrid_weights: bfloat16 [2, 2048, 3, 128, 128], P('sec', 'blk'), may hold values from -0.3125 to 0.3125
Outputs:
- new_state: float32 [2, 64, 512, 512], P('sec', None, 'blk')
- coupled: bfloat16 [2, 8, 512, 512], P('sec', None, 'blk')
The draws below stay inside these ranges and needn't reach their ends.
Inputs may be any that keep to these rules, and one draw needn't show every extreme that they name: `sources`: an entry of a destination tile in block b names a tile of the other component whose block lies within 2 blocks of b, counted cyclically over the blocks; the distance 2 occurs on both sides in every block.
All inputs are finite; a program needn't handle non-finite values. No bound on the sum of `land_mask` on one device may be relied on, other than what follows from the above.
Results may differ from the reference program's by a relative error of at most 0.0048.
Values may be sent and summed in bfloat16 or wider, within the bound.
No kernel may reach another device: no remote copies, remote signals or barrier semaphores. Data moves between devices by JAX's collectives and lax.ppermute only.
A program may use at most 128 MiB of HBM per device.

```python
import jax
import jax.numpy as jnp
from jax import lax

LEV = 64
K = 8
ROWS = 32
COLS = 512
TC = 128
OV = 3
REACH = 2
NSTEP = 4
NR = 512
TILES = 2048
N_BLK = 16


def draw_sources(key, part):
    first, second = jax.random.split(jax.random.fold_in(key, 11))
    tiles_block = ROWS * COLS // TC
    count = N_BLK * tiles_block
    offsets = jax.random.randint(first, (2, count, OV), -REACH, REACH + 1)
    chosen = jax.random.randint(second, (2, count, OV), 0, tiles_block)
    local_tile = jnp.arange(count) % tiles_block
    lead_slot = jnp.arange(OV)
    upper = (local_tile[None, :, None] == 0) & (lead_slot[None, None, :] == 0)
    lower = (local_tile[None, :, None] == 0) & (lead_slot[None, None, :] == 1)
    offsets = jnp.where(upper, REACH, offsets)
    offsets = jnp.where(lower, -REACH, offsets)
    dest_block = jnp.arange(count) // tiles_block
    src_block = (dest_block[None, :, None] + offsets) % N_BLK
    return (src_block * tiles_block + chosen).astype(jnp.int32)


def plant(result, rng, least, largest):
    extent = result.shape
    index_at = [jax.random.randint(jax.random.fold_in(rng, axis), (), 0, extent[axis]) for axis in range(len(extent))]
    result = result.at[tuple(index_at)].set(least)
    longest = extent.index(max(extent))
    index_at[longest] = (index_at[longest] + 1) % extent[longest]
    return result.at[tuple(index_at)].set(largest)


def block_levels(stream_key, extent, pieces, least, top_value):
    level = 1.0
    for axis_at, parts in pieces:
        heights = jax.random.uniform(jax.random.fold_in(jax.random.fold_in(stream_key, 6), axis_at), (parts,), jnp.float32, least / len(pieces), top_value / len(pieces))
        level = level * jnp.repeat(jnp.exp(heights), extent[axis_at] // parts).reshape((-1,) + (1,) * (len(extent) - 1 - axis_at))
    return level


def scatter_about(own_key, extent, deviation, most, cuts=(), held_as=jnp.bfloat16):
    drawn = jax.random.normal(own_key, extent, jnp.float32) * deviation
    if len(cuts) > 0:
        drawn = block_levels(own_key, extent, cuts, -0.22, 0.18) * drawn
    return jnp.clip(drawn, min=-most, max=most).astype(held_as)


def setup_inputs(seed: int = 0) -> dict:
    seeds = jax.random.split(jax.random.key(seed), 10)
    column_state = scatter_about(seeds[0], (2, LEV, NR, COLS), 1.0, 6.0, ((0, 2), (2, 16)), jnp.float32)
    forcing = scatter_about(seeds[1], (2, K, NR, COLS), 1.0, 6.0, ((0, 2), (2, 16)))
    couple_gain = scatter_about(seeds[2], (2, LEV, K), K ** -0.5, 2.0, ((0, 2),))
    diffusion = jnp.clip(0.2 + 0.03999999 * jax.random.uniform(seeds[3], (2, LEV), jnp.float32) ** block_levels(seeds[3], (2, LEV), ((0, 2),), -0.2, 0.2), 0.2, 0.24)
    mixing = scatter_about(seeds[4], (2, LEV, LEV), LEV ** -0.5, 0.75, ((0, 2),), jnp.float32)
    export_map = scatter_about(seeds[5], (2, K, LEV), LEV ** -0.5, 0.75, ((0, 2),), jnp.float32)
    land_mask = plant((jax.random.randint(seeds[6], (NR, COLS), 0, 10) < 7).astype(jnp.int32), jax.random.fold_in(seeds[6], 1), 0, 1)
    sources = draw_sources(jax.random.fold_in(seeds[9], 71), 0)
    regrid_weights = scatter_about(seeds[8], (2, TILES, OV, TC, TC), (OV * TC) ** -0.5, 0.3125, ((0, 2), (1, 16)))
    return {"column_state": column_state, "forcing": forcing, "couple_gain": couple_gain, "diffusion": diffusion, "mixing": mixing, "export_map": export_map, "land_mask": land_mask, "sources": sources, "regrid_weights": regrid_weights}


def laplace(field):
    padded = jnp.pad(field, ((0, 0), (1, 1), (0, 0)))
    return padded[:, 2:] + padded[:, :-2] + jnp.roll(field, 1, 2) + jnp.roll(field, -1, 2) - 4.0 * field


def dynamics(field, wetness, diffuse_rate, mixing):
    for step_index in range(NSTEP):
        field = field + wetness[None] * diffuse_rate[:, None, None] * laplace(field)
        field = 0.5 * (field + jnp.einsum("ij,jrc->irc", mixing, field, precision=lax.Precision.HIGHEST))
    return field


def regrid_block(pair):
    picked, weights = pair
    return jnp.einsum("ktoc,tocd->ktd", picked.astype(jnp.float32), weights.astype(jnp.float32), precision=lax.Precision.HIGHEST)


def reference(column_state, forcing, couple_gain, diffusion, mixing, export_map, land_mask, sources, regrid_weights):
    ocean_wet = land_mask.astype(jnp.float32)
    states = []
    surfaces = []
    for section in range(2):
        driven = column_state[section] + jnp.einsum("lk,krc->lrc", couple_gain[section].astype(jnp.float32), forcing[section].astype(jnp.float32), precision=lax.Precision.HIGHEST)
        wetness = ocean_wet if section == 1 else jnp.ones_like(ocean_wet)
        field = dynamics(driven, wetness, diffusion[section], mixing[section])
        states.append(field)
        surface = jnp.tanh(jnp.einsum("kl,lrc->krc", export_map[section], field, precision=lax.Precision.HIGHEST))
        surfaces.append(surface.astype(jnp.bfloat16))
    coupled = []
    blocks = NR // ROWS
    tiles_block = ROWS * COLS // TC
    for section in range(2):
        partner = surfaces[1 - section].reshape(K, NR * COLS // TC, TC)
        picked = jnp.take(partner, sources[section].reshape(-1).astype(jnp.int32), axis=1)
        picked = picked.reshape(K, blocks, tiles_block, OV, TC).transpose(1, 0, 2, 3, 4)
        weights = regrid_weights[section].reshape(blocks, tiles_block, OV, TC, TC)
        mixed = lax.map(regrid_block, (picked, weights))
        mixed = mixed.transpose(1, 0, 2, 3).reshape(K, NR, COLS)
        coupled.append(mixed.astype(jnp.bfloat16))
    return jnp.stack(states), jnp.stack(coupled)
```

```python
import jax
import jax.numpy as jnp
from jax import lax
from jax.experimental import pallas as pl
from jax.experimental.pallas import tpu as pltpu
from jax.sharding import PartitionSpec as P

TC = 128
OV = 3
REACH = 2
NSTEP = 4
EDGE = NSTEP
F32 = jnp.float32
BF16 = jnp.bfloat16
VMEM = pltpu.VMEM
MIB = 2**20


def split(value):
    high = value.astype(BF16)
    return high, (value - high.astype(F32)).astype(BF16)


def column(row):
    n = row.shape[1]
    eye = lax.broadcasted_iota(jnp.int32, (n, n), 0) == lax.broadcasted_iota(jnp.int32, (n, n), 1)
    return jnp.sum(jnp.where(eye, jnp.broadcast_to(row, (n, n)), 0.0), axis=1, keepdims=True)


def stacked(matrix):
    high, low = split(matrix)
    return jnp.concatenate([high, high, low], axis=1)


def mixers(mixing, export_map):
    n = mixing.shape[0]
    eye = lax.broadcasted_iota(jnp.int32, (n, n), 0) == lax.broadcasted_iota(jnp.int32, (n, n), 1)
    step = 0.5 * (jnp.where(eye, 1.0, 0.0) + mixing)
    out = jnp.dot(export_map, step, precision=lax.Precision.HIGHEST, preferred_element_type=F32)
    return stacked(jnp.concatenate([step, out], axis=0))


def rows_of(blocks, first, size, stride):
    return jnp.concatenate([block[pl.ds(first, size, stride=stride), :] for block in blocks], axis=1)


def blocks_of(ref):
    return [ref.at[index] for index in range(ref.shape[0])]


def diffused(here, above, below, wet, rate, rest):
    columns = here.shape[1]
    near = above + below + pltpu.roll(here, 1, 1) + pltpu.roll(here, columns - 1, 1)
    return jnp.where(wet > 0.0, rate * near + rest * here, here)


def mixed(factor, value):
    high, low = split(value)
    return jnp.dot(factor, jnp.concatenate([high, low, high], axis=0), preferred_element_type=F32)


def load_force(forcing_ref, force):
    value = forcing_ref[...].astype(F32)
    for index in range(force.shape[0]):
        force[index] = value[:, index * TC : (index + 1) * TC]


def edge_kernel(*refs):
    forcing_ref, gain_ref, wet_ref, down_ref, up_ref, force = refs[-6:]
    blocks = (len(refs) - 6) // 2
    top_refs = refs[:blocks]
    bottom_refs = refs[blocks : 2 * blocks]
    levels, fields = gain_ref.shape
    columns = forcing_ref.shape[1]
    rows = forcing_ref.shape[0] // fields
    load_force(forcing_ref, force)
    gain = gain_ref[...]
    for state_refs, out_ref, first, inside in (
        (top_refs, down_ref, 0, 0),
        (bottom_refs, up_ref, rows - EDGE, 8 - EDGE),
    ):
        state = [ref.reshape(levels * 8, TC) for ref in state_refs]
        for row in range(EDGE):
            pushed = rows_of(blocks_of(force), first + row, fields, rows).astype(BF16)
            value = rows_of(state, inside + row, levels, 8) + jnp.dot(
                gain, pushed, preferred_element_type=F32
            )
            out_ref[levels * row : levels * (row + 1), :] = value.astype(BF16)
        out_ref[levels * EDGE :, :] = jnp.concatenate(
            [wet_ref[first : first + EDGE, :], jnp.zeros((16 - EDGE, columns), F32)], axis=0
        ).astype(BF16)


def inner_kernel(*refs):
    state_refs = refs[:-12]
    forcing_ref, gain_ref, rate_ref, mixing_ref, export_ref, wet_ref = refs[-12:-6]
    final_ref, edge_ref, surface_ref, even, odd, force = refs[-6:]
    levels, fields = gain_ref.shape
    rows, columns = wet_ref.shape
    load_force(forcing_ref, force)
    gain = gain_ref[...]

    @pl.loop(0, rows // 4)
    def _(group):
        for part in range(4):
            row = group * 4 + part
            pushed = rows_of(blocks_of(force), row, fields, rows).astype(BF16)
            even[row] = rows_of(state_refs, row, levels, rows) + jnp.dot(
                gain, pushed, preferred_element_type=F32
            )

    rate = column(rate_ref[...])
    rest = 1.0 - 4.0 * rate
    factor = mixers(mixing_ref[...], export_ref[...])
    step_factor = factor[:levels]
    for step in range(1, NSTEP + 1):
        source, target = (even, odd) if step % 2 else (odd, even)
        last = step == NSTEP

        @pl.loop(0, (rows - 2 * step) // 2)
        def _(pair, source=source, target=target, step=step, last=last):
            for part in range(2):
                row = step + 2 * pair + part
                value = diffused(
                    source[row],
                    source[row - 1],
                    source[row + 1],
                    wet_ref[pl.ds(row, 1), :],
                    rate,
                    rest,
                )
                result = mixed(factor if last else step_factor, value)
                if last:
                    final_ref[row - EDGE] = result[:levels]
                    surface = jnp.tanh(result[levels:]).astype(BF16)
                    per_row = columns // TC
                    for tile in range(per_row):
                        surface_ref[(row - EDGE) * per_row + tile] = surface[
                            :, tile * TC : (tile + 1) * TC
                        ]
                else:
                    target[row] = result

    for step in range(NSTEP):
        source = odd if step % 2 else even
        edge_ref[0, step, 0] = source[step]
        edge_ref[0, step, 1] = source[step + 1]
        edge_ref[1, step, 0] = source[rows - 2 - step]
        edge_ref[1, step, 1] = source[rows - 1 - step]


def outer_kernel(
    low_ref,
    high_ref,
    edge_ref,
    rate_ref,
    mixing_ref,
    export_ref,
    wet_ref,
    final_ref,
    surface_ref,
    even,
    odd,
    wet,
):
    levels = mixing_ref.shape[0]
    rows, columns = wet_ref.shape
    per_row = columns // TC
    rate = column(rate_ref[...])
    rest = 1.0 - 4.0 * rate
    factor = mixers(mixing_ref[...], export_ref[...])
    step_factor = factor[:levels]
    wet[0, 0:EDGE, :] = low_ref[levels * EDGE :, :].astype(F32)[0:EDGE]
    wet[0, EDGE : 2 * EDGE, :] = wet_ref[0:EDGE, :]
    wet[1, 0:EDGE, :] = wet_ref[rows - EDGE : rows, :]
    wet[1, EDGE : 2 * EDGE, :] = high_ref[levels * EDGE :, :].astype(F32)[0:EDGE]
    for row in range(EDGE):
        even[0, row] = low_ref[levels * row : levels * (row + 1), :].astype(F32)
        even[1, row + 2] = high_ref[levels * row : levels * (row + 1), :].astype(F32)
    for step in range(1, NSTEP + 1):
        source, target = (even, odd) if step % 2 else (odd, even)
        last = step == NSTEP
        for item in range(2):
            source[0, EDGE + item] = edge_ref[0, step - 1, item]
            source[1, item] = edge_ref[1, step - 1, item]
        for side in range(2):
            first_wet = step if side == 0 else NSTEP - step
            shift = 0 if side == 0 else 2

            @pl.loop(0, EDGE // 2)
            def _(pair):
                for part in range(2):
                    row = 2 * pair + part
                    value = diffused(
                        source[side, row + 1],
                        source[side, row],
                        source[side, row + 2],
                        wet[side, pl.ds(first_wet + row, 1), :],
                        rate,
                        rest,
                    )
                    result = mixed(factor if last else step_factor, value)
                    if last:
                        final_ref[side, row] = result[:levels]
                        surface = jnp.tanh(result[levels:]).astype(BF16)
                        for tile in range(per_row):
                            surface_ref[(side * EDGE + row) * per_row + tile] = surface[
                                :, tile * TC : (tile + 1) * TC
                            ]
                    else:
                        target[side, row + shift] = result


def write_kernel(inner_ref, outer_ref, state_ref):
    levels = inner_ref.shape[1]
    rows = inner_ref.shape[0] + 2 * EDGE

    for row in range(EDGE):
        state_ref[pl.ds(row, levels, stride=rows), :] = outer_ref[0, row]
        state_ref[pl.ds(rows - EDGE + row, levels, stride=rows), :] = outer_ref[1, row]

    @pl.loop(0, rows - 2 * EDGE)
    def _(row):
        state_ref[pl.ds(row + EDGE, levels, stride=rows), :] = inner_ref[row]


def regrid_kernel(position_ref, *refs):
    inner_refs = refs[0:6]
    outer_refs = refs[6:12]
    weight_ref, out_ref, held, sums, sems = refs[12:]
    step = pl.program_id(0)
    tiles_step = weight_ref.shape[0]
    inner_tiles = inner_refs[0].shape[0]
    edge_tiles = outer_refs[0].shape[0] // 2
    tiles = inner_tiles + 2 * edge_tiles
    fields = inner_refs[0].shape[1]
    columns = out_ref.shape[1]
    rows = out_ref.shape[0] // fields
    per_row = columns // TC

    @pl.when(step == 0)
    def _():
        copies = []
        for slot in range(6):
            start = slot * tiles
            for piece, (source, place) in enumerate(
                (
                    (inner_refs[slot], pl.ds(start + edge_tiles, inner_tiles)),
                    (outer_refs[slot].at[pl.ds(0, edge_tiles)], pl.ds(start, edge_tiles)),
                    (
                        outer_refs[slot].at[pl.ds(edge_tiles, edge_tiles)],
                        pl.ds(start + edge_tiles + inner_tiles, edge_tiles),
                    ),
                )
            ):
                copies.append(
                    pltpu.make_async_copy(source, held.at[place], sems.at[slot, piece])
                )
        for copy in copies:
            copy.start()
        for copy in copies:
            copy.wait()

    for pair in range(tiles_step // 2):
        lefts = []
        for item in range(2):
            base = (step * tiles_step + 2 * pair + item) * OV
            lefts.append(
                jnp.concatenate([held[position_ref[base + slot]] for slot in range(OV)], axis=1)
            )
        left = jnp.concatenate(lefts, axis=0)
        right = jnp.concatenate([weight_ref[2 * pair], weight_ref[2 * pair + 1]], axis=1)
        result = jnp.dot(left, right, preferred_element_type=F32)
        for item in range(2):
            tile = 2 * pair + item
            row = step * (tiles_step // per_row) + tile // per_row
            sums[tile % per_row, pl.ds(row, fields, stride=rows), :] = result[
                item * fields : (item + 1) * fields, item * TC : (item + 1) * TC
            ]

    @pl.when(step == pl.num_programs(0) - 1)
    def _():
        for index in range(per_row):
            out_ref[:, index * TC : (index + 1) * TC] = sums[index].astype(BF16)


def on_device(
    column_state,
    forcing,
    couple_gain,
    diffusion,
    mixing,
    export_map,
    land_mask,
    sources,
    regrid_weights,
):
    section = lax.axis_index("sec")
    shard = lax.axis_index("blk")
    count = lax.axis_size("blk")
    _, levels, rows, columns = column_state.shape
    fields = forcing.shape[1]
    tiles = rows * columns // TC
    per_row = columns // TC
    inner_rows = rows - 2 * EDGE
    inner_tiles = inner_rows * per_row
    outer_tiles = 2 * EDGE * per_row
    state = column_state[0]
    force = forcing[0].reshape(fields * rows, columns)
    gain = couple_gain[0]
    rate = diffusion
    mixer = mixing[0]
    export = export_map[0]
    wetness = jnp.where(section == 1, land_mask.astype(F32), jnp.ones(land_mask.shape, F32))
    whole = pl.BlockSpec(memory_space=VMEM)

    payload = levels * EDGE + 16
    down, up = pl.pallas_call(
        edge_kernel,
        grid=(1,),
        in_specs=[
            pl.BlockSpec((levels, 8, TC), lambda i, j=index, k=k: (0, k, j))
            for k in (0, rows // 8 - 1)
            for index in range(per_row)
        ]
        + [
            pl.BlockSpec((fields * rows, columns), lambda i: (0, 0)),
            pl.BlockSpec((levels, fields), lambda i: (0, 0)),
            pl.BlockSpec((rows, columns), lambda i: (0, 0)),
        ],
        out_specs=[pl.BlockSpec((payload, columns), lambda i: (0, 0))] * 2,
        out_shape=[jax.ShapeDtypeStruct((payload, columns), BF16)] * 2,
        scratch_shapes=[VMEM((per_row, fields * rows, TC), F32)],
        compiler_params=pltpu.CompilerParams(vmem_limit_bytes=16 * MIB),
        cost_estimate=pl.CostEstimate(flops=10**7, bytes_accessed=3 * MIB, transcendentals=0),
        name="edges",
    )(*[state] * (2 * per_row), force, gain, wetness)
    upward = [(i, i + 1) for i in range(count - 1)]
    downward = [(i + 1, i) for i in range(count - 1)]
    low = lax.ppermute(up, "blk", upward)
    high = lax.ppermute(down, "blk", downward)

    inner_final, edges, inner_surface = pl.pallas_call(
        inner_kernel,
        grid=(1,),
        in_specs=[
            pl.BlockSpec((levels * rows, TC), lambda i, j=index: (0, j)) for index in range(per_row)
        ]
        + [whole] * 6,
        out_specs=[whole] * 3,
        out_shape=[
            jax.ShapeDtypeStruct((inner_rows, levels, columns), F32),
            jax.ShapeDtypeStruct((2, NSTEP, 2, levels, columns), F32),
            jax.ShapeDtypeStruct((inner_tiles, fields, TC), BF16),
        ],
        scratch_shapes=[
            VMEM((rows, levels, columns), F32),
            VMEM((rows, levels, columns), F32),
            VMEM((per_row, fields * rows, TC), F32),
        ],
        compiler_params=pltpu.CompilerParams(vmem_limit_bytes=32 * MIB),
        cost_estimate=pl.CostEstimate(flops=10**10, bytes_accessed=20 * MIB, transcendentals=0),
        name="inner",
    )(*[state.reshape(levels * rows, columns)] * per_row, force, gain, rate, mixer, export, wetness)

    outer_final, outer_surface = pl.pallas_call(
        outer_kernel,
        in_specs=[whole] * 7,
        out_specs=[whole] * 2,
        out_shape=[
            jax.ShapeDtypeStruct((2, EDGE, levels, columns), F32),
            jax.ShapeDtypeStruct((outer_tiles, fields, TC), BF16),
        ],
        scratch_shapes=[
            VMEM((2, EDGE + 2, levels, columns), F32),
            VMEM((2, EDGE + 2, levels, columns), F32),
            VMEM((2, 2 * EDGE, columns), F32),
        ],
        compiler_params=pltpu.CompilerParams(vmem_limit_bytes=16 * MIB),
        cost_estimate=pl.CostEstimate(flops=3 * 10**9, bytes_accessed=4 * MIB, transcendentals=0),
        name="outer",
    )(low, high, edges, rate, mixer, export, wetness)

    new_state = pl.pallas_call(
        write_kernel,
        grid=(per_row,),
        in_specs=[
            pl.BlockSpec((inner_rows, levels, TC), lambda j: (0, 0, j)),
            pl.BlockSpec((2, EDGE, levels, TC), lambda j: (0, 0, 0, j)),
        ],
        out_specs=pl.BlockSpec((levels * rows, TC), lambda j: (0, j)),
        out_shape=jax.ShapeDtypeStruct((levels * rows, columns), F32),
        compiler_params=pltpu.CompilerParams(vmem_limit_bytes=16 * MIB),
        cost_estimate=pl.CostEstimate(flops=0, bytes_accessed=8 * MIB, transcendentals=0),
        name="write",
    )(inner_final, outer_final)

    section_count = lax.axis_size("sec")
    across = [(i, section_count - 1 - i) for i in range(section_count)]
    later = [(i, (i + 2) % count) for i in range(count)]
    earlier = [(i, (i - 2) % count) for i in range(count)]
    mates = [(i, i ^ 1) for i in range(count)]

    def gathered(surface):
        here = lax.ppermute(surface, "sec", across)
        before = lax.ppermute(here, "blk", later)
        after = lax.ppermute(here, "blk", earlier)
        own = [before, here, after]
        other = [lax.ppermute(piece, "blk", mates) for piece in own]
        return own + other

    inner_pieces = gathered(inner_surface)
    outer_pieces = gathered(outer_surface)

    core = shard % 2
    wanted = sources.reshape(-1)
    away = wanted // tiles - (shard - core) + 2
    away = away % count
    same_core = away % 2 == core
    positions = (jnp.where(same_core, 0, 3) + away // 2) * tiles + wanted % tiles

    tiles_step = 16
    weights = regrid_weights.reshape(tiles, OV * TC, TC)
    anywhere = pl.BlockSpec(memory_space=pl.ANY)
    coupled = pl.pallas_call(
        regrid_kernel,
        grid_spec=pltpu.PrefetchScalarGridSpec(
            num_scalar_prefetch=1,
            grid=(tiles // tiles_step,),
            in_specs=[anywhere] * 12
            + [pl.BlockSpec((tiles_step, OV * TC, TC), lambda i, p: (i, 0, 0))],
            out_specs=pl.BlockSpec((fields * rows, columns), lambda i, p: (0, 0)),
            scratch_shapes=[
                VMEM((6 * tiles, fields, TC), BF16),
                VMEM((per_row, fields * rows, TC), F32),
                pltpu.SemaphoreType.DMA((6, 3)),
            ],
        ),
        out_shape=jax.ShapeDtypeStruct((fields * rows, columns), BF16),
        compiler_params=pltpu.CompilerParams(vmem_limit_bytes=16 * MIB),
        cost_estimate=pl.CostEstimate(flops=10**9, bytes_accessed=16 * MIB, transcendentals=0),
        name="regrid",
    )(positions, *inner_pieces, *outer_pieces, weights)

    return (
        new_state.reshape(1, levels, rows, columns),
        coupled.reshape(1, fields, rows, columns),
    )


def solution(mesh):
    in_specs = (
        P("sec", None, "blk", None),
        P("sec", None, "blk", None),
        P("sec", None, None),
        P("sec", None),
        P("sec", None, None),
        P("sec", None, None),
        P("blk", None),
        P("sec", "blk", None),
        P("sec", "blk", None, None, None),
    )
    out_specs = (P("sec", None, "blk", None), P("sec", None, "blk", None))
    return jax.shard_map(
        on_device, mesh=mesh, in_specs=in_specs, out_specs=out_specs, check_vma=False
    )
```

```python
import jax
import jax.numpy as jnp
from jax import lax
from jax.experimental import pallas as pl
from jax.experimental.pallas import tpu as pltpu
from jax.sharding import PartitionSpec as P

TC = 128
OV = 3
REACH = 2
NSTEP = 4
EDGE = NSTEP
F32 = jnp.float32
BF16 = jnp.bfloat16
VMEM = pltpu.VMEM
MIB = 2**20


def split(value):
    high = value.astype(BF16)
    return high, (value - high.astype(F32)).astype(BF16)


def column(row):
    n = row.shape[1]
    eye = lax.broadcasted_iota(jnp.int32, (n, n), 0) == lax.broadcasted_iota(jnp.int32, (n, n), 1)
    return jnp.sum(jnp.where(eye, jnp.broadcast_to(row, (n, n)), 0.0), axis=1, keepdims=True)


def stacked(matrix):
    high, low = split(matrix)
    return jnp.concatenate([high, high, low], axis=1)


def mixers(mixing, export_map):
    n = mixing.shape[0]
    eye = lax.broadcasted_iota(jnp.int32, (n, n), 0) == lax.broadcasted_iota(jnp.int32, (n, n), 1)
    step = 0.5 * (jnp.where(eye, 1.0, 0.0) + mixing)
    out = jnp.dot(export_map, step, precision=lax.Precision.HIGHEST, preferred_element_type=F32)
    return stacked(jnp.concatenate([step, out], axis=0))


def rows_of(blocks, first, size, stride):
    return jnp.concatenate([block[pl.ds(first, size, stride=stride), :] for block in blocks], axis=1)


def driven(gain, pushed):
    return lax.dot_general(gain, pushed, (((0,), (0,)), ((), ())), preferred_element_type=F32)


def wetness_of(mask):
    return jnp.where((mask > 0) | (lax.axis_index("sec") != 1), 1.0, 0.0)


def blocks_of(ref):
    return [ref.at[index] for index in range(ref.shape[0])]


def diffused(here, above, below, wet, rate, rest):
    columns = here.shape[1]
    near = above + below + pltpu.roll(here, 1, 1) + pltpu.roll(here, columns - 1, 1)
    return jnp.where(wet > 0.0, rate * near + rest * here, here)


def mixed(factor, value):
    high, low = split(value)
    return jnp.dot(factor, jnp.concatenate([high, low, high], axis=0), preferred_element_type=F32)


def load_force(forcing_ref, force):
    value = forcing_ref[...].astype(F32)
    for index in range(force.shape[0]):
        force[index] = value[:, index * TC : (index + 1) * TC]


def edge_kernel(*refs):
    forcing_ref, gain_ref, mask_ref, down_ref, up_ref, force = refs[-6:]
    blocks = (len(refs) - 6) // 2
    top_refs = refs[:blocks]
    bottom_refs = refs[blocks : 2 * blocks]
    fields, levels = gain_ref.shape
    columns = forcing_ref.shape[1]
    rows = forcing_ref.shape[0] // fields
    load_force(forcing_ref, force)
    gain = gain_ref[...]
    for state_refs, out_ref, first, inside in (
        (top_refs, down_ref, 0, 0),
        (bottom_refs, up_ref, rows - EDGE, 8 - EDGE),
    ):
        state = [ref.reshape(levels * 8, TC) for ref in state_refs]
        for row in range(EDGE):
            pushed = rows_of(blocks_of(force), first + row, fields, rows).astype(BF16)
            value = rows_of(state, inside + row, levels, 8) + driven(gain, pushed)
            out_ref[levels * row : levels * (row + 1), :] = value.astype(BF16)
        out_ref[levels * EDGE :, :] = jnp.concatenate(
            [wetness_of(mask_ref[first : first + EDGE, :]), jnp.zeros((16 - EDGE, columns), F32)], axis=0
        ).astype(BF16)


def inner_kernel(*refs):
    state_refs = refs[:-13]
    forcing_ref, gain_ref, rate_ref, mixing_ref, export_ref, mask_ref = refs[-13:-7]
    final_ref, edge_ref, surface_ref, even, odd, force, wet_ref = refs[-7:]
    fields, levels = gain_ref.shape
    rows, columns = wet_ref.shape
    load_force(forcing_ref, force)
    wet_ref[...] = wetness_of(mask_ref[...])
    gain = gain_ref[...]

    @pl.loop(0, rows // 4)
    def _(group):
        for part in range(4):
            row = group * 4 + part
            pushed = rows_of(blocks_of(force), row, fields, rows).astype(BF16)
            even[row] = rows_of(state_refs, row, levels, rows) + driven(gain, pushed)

    rate = column(rate_ref[...])
    rest = 1.0 - 4.0 * rate
    factor = mixers(mixing_ref[...], export_ref[...])
    step_factor = factor[:levels]
    for step in range(1, NSTEP + 1):
        source, target = (even, odd) if step % 2 else (odd, even)
        last = step == NSTEP

        todo = rows - 2 * step
        at_once = max(n for n in (1, 2, 3, 4, 5) if todo % n == 0)

        @pl.loop(0, todo // at_once)
        def _(group, source=source, target=target, step=step, last=last, at_once=at_once):
            for part in range(at_once):
                row = step + at_once * group + part
                value = diffused(
                    source[row],
                    source[row - 1],
                    source[row + 1],
                    wet_ref[pl.ds(row, 1), :],
                    rate,
                    rest,
                )
                result = mixed(factor if last else step_factor, value)
                if last:
                    final_ref[row - EDGE] = result[:levels]
                    surface = jnp.tanh(result[levels:]).astype(BF16)
                    per_row = columns // TC
                    for tile in range(per_row):
                        surface_ref[(row - EDGE) * per_row + tile] = surface[
                            :, tile * TC : (tile + 1) * TC
                        ]
                else:
                    target[row] = result

    for step in range(NSTEP):
        source = odd if step % 2 else even
        edge_ref[0, step, 0] = source[step]
        edge_ref[0, step, 1] = source[step + 1]
        edge_ref[1, step, 0] = source[rows - 2 - step]
        edge_ref[1, step, 1] = source[rows - 1 - step]


def outer_kernel(
    low_ref,
    high_ref,
    edge_ref,
    rate_ref,
    mixing_ref,
    export_ref,
    mask_ref,
    inner_ref,
    final_ref,
    surface_ref,
    even,
    odd,
    wet,
):
    levels = mixing_ref.shape[0]
    rows, columns = mask_ref.shape
    inner_tiles = inner_ref.shape[0]
    per_row = columns // TC
    rate = column(rate_ref[...])
    rest = 1.0 - 4.0 * rate
    factor = mixers(mixing_ref[...], export_ref[...])
    step_factor = factor[:levels]
    wet[0, 0:EDGE, :] = low_ref[levels * EDGE :, :].astype(F32)[0:EDGE]
    wet[0, EDGE : 2 * EDGE, :] = wetness_of(mask_ref[0:EDGE, :])
    wet[1, 0:EDGE, :] = wetness_of(mask_ref[rows - EDGE : rows, :])
    surface_ref[pl.ds(EDGE * per_row, inner_tiles)] = inner_ref[...]
    wet[1, EDGE : 2 * EDGE, :] = high_ref[levels * EDGE :, :].astype(F32)[0:EDGE]
    for row in range(EDGE):
        even[0, row] = low_ref[levels * row : levels * (row + 1), :].astype(F32)
        even[1, row + 2] = high_ref[levels * row : levels * (row + 1), :].astype(F32)
    for step in range(1, NSTEP + 1):
        source, target = (even, odd) if step % 2 else (odd, even)
        last = step == NSTEP
        for item in range(2):
            source[0, EDGE + item] = edge_ref[0, step - 1, item]
            source[1, item] = edge_ref[1, step - 1, item]
        for side in range(2):
            first_wet = step if side == 0 else NSTEP - step
            shift = 0 if side == 0 else 2

            @pl.loop(0, 1)
            def _(pair):
                for part in range(EDGE):
                    row = EDGE * pair + part
                    value = diffused(
                        source[side, row + 1],
                        source[side, row],
                        source[side, row + 2],
                        wet[side, pl.ds(first_wet + row, 1), :],
                        rate,
                        rest,
                    )
                    result = mixed(factor if last else step_factor, value)
                    if last:
                        final_ref[side, row] = result[:levels]
                        surface = jnp.tanh(result[levels:]).astype(BF16)
                        for tile in range(per_row):
                            surface_ref[(side * (rows - EDGE) + row) * per_row + tile] = surface[
                                :, tile * TC : (tile + 1) * TC
                            ]
                    else:
                        target[side, row + shift] = result


def write_kernel(inner_ref, outer_ref, state_ref):
    levels = inner_ref.shape[1]
    rows = inner_ref.shape[0] + 2 * EDGE

    for row in range(EDGE):
        state_ref[pl.ds(row, levels, stride=rows), :] = outer_ref[0, row]
        state_ref[pl.ds(rows - EDGE + row, levels, stride=rows), :] = outer_ref[1, row]

    @pl.loop(0, rows - 2 * EDGE)
    def _(row):
        state_ref[pl.ds(row + EDGE, levels, stride=rows), :] = inner_ref[row]


def regrid_kernel(position_ref, *refs):
    piece_refs = refs[0:6]
    weight_ref, out_ref, held, weights, sums, piece_sems, weight_sems = refs[6:]
    tiles, fields, _ = piece_refs[0].shape
    chunks = weight_sems.shape[0]
    tiles_chunk = tiles // chunks
    per_row, total_rows, _ = sums.shape
    rows = total_rows // fields

    def weight_copy(chunk):
        part = pl.ds(chunk * tiles_chunk, tiles_chunk)
        return pltpu.make_async_copy(weight_ref.at[part], weights.at[part], weight_sems.at[chunk])

    copies = [
        pltpu.make_async_copy(source, held.at[pl.ds(slot * tiles, tiles)], piece_sems.at[slot])
        for slot, source in enumerate(piece_refs)
    ]
    for copy in copies:
        copy.start()
    for chunk in range(chunks):
        weight_copy(chunk).start()
    for copy in copies:
        copy.wait()

    @pl.loop(0, chunks)
    def _(chunk):
        weight_copy(chunk).wait()
        for pair in range(tiles_chunk // 2):
            first = chunk * tiles_chunk + 2 * pair
            lefts = []
            for item in range(2):
                base = (first + item) * OV
                lefts.append(
                    jnp.concatenate([held[position_ref[base + slot]] for slot in range(OV)], axis=1)
                )
            left = jnp.concatenate(lefts, axis=0)
            right = jnp.concatenate([weights[first], weights[first + 1]], axis=1)
            result = jnp.dot(left, right, preferred_element_type=F32)
            for item in range(2):
                tile = 2 * pair + item
                row = chunk * (tiles_chunk // per_row) + tile // per_row
                sums[tile % per_row, pl.ds(row, fields, stride=rows), :] = result[
                    item * fields : (item + 1) * fields, item * TC : (item + 1) * TC
                ]

    for index in range(per_row):
        out_ref[:, index * TC : (index + 1) * TC] = sums[index].astype(BF16)


def in_hbm(value):
    return pltpu.with_memory_space_constraint(value, pltpu.HBM)


def on_device(
    column_state,
    forcing,
    couple_gain,
    diffusion,
    mixing,
    export_map,
    land_mask,
    sources,
    regrid_weights,
):
    shard = lax.axis_index("blk")
    count = lax.axis_size("blk")
    _, levels, rows, columns = column_state.shape
    fields = forcing.shape[1]
    tiles = rows * columns // TC
    per_row = columns // TC
    inner_rows = rows - 2 * EDGE
    inner_tiles = inner_rows * per_row
    state = in_hbm(column_state[0])
    force = in_hbm(forcing.reshape(fields * rows, columns))
    gain = in_hbm(couple_gain[0].T)
    land_mask = in_hbm(land_mask)
    rate = diffusion
    mixer = mixing[0]
    export = export_map[0]
    whole = pl.BlockSpec(memory_space=VMEM)

    payload = levels * EDGE + 16
    down, up = pl.pallas_call(
        edge_kernel,
        grid=(1,),
        in_specs=[
            pl.BlockSpec((levels, 8, TC), lambda i, j=index, k=k: (0, k, j))
            for k in (0, rows // 8 - 1)
            for index in range(per_row)
        ]
        + [
            pl.BlockSpec((fields * rows, columns), lambda i: (0, 0)),
            pl.BlockSpec((fields, levels), lambda i: (0, 0)),
            pl.BlockSpec((rows, columns), lambda i: (0, 0)),
        ],
        out_specs=[pl.BlockSpec((payload, columns), lambda i: (0, 0))] * 2,
        out_shape=[jax.ShapeDtypeStruct((payload, columns), BF16)] * 2,
        scratch_shapes=[VMEM((per_row, fields * rows, TC), F32)],
        compiler_params=pltpu.CompilerParams(vmem_limit_bytes=16 * MIB),
        cost_estimate=pl.CostEstimate(flops=10**7, bytes_accessed=3 * MIB, transcendentals=0),
        name="edges",
    )(*[state] * (2 * per_row), force, gain, land_mask)
    upward = [(i, i + 1) for i in range(count - 1)]
    downward = [(i + 1, i) for i in range(count - 1)]
    low = lax.ppermute(up, "blk", upward)
    high = lax.ppermute(down, "blk", downward)

    inner_final, edges, inner_surface = pl.pallas_call(
        inner_kernel,
        grid=(1,),
        in_specs=[
            pl.BlockSpec((levels * rows, TC), lambda i, j=index: (0, j)) for index in range(per_row)
        ]
        + [whole] * 6,
        out_specs=[whole] * 3,
        out_shape=[
            jax.ShapeDtypeStruct((inner_rows, levels, columns), F32),
            jax.ShapeDtypeStruct((2, NSTEP, 2, levels, columns), F32),
            jax.ShapeDtypeStruct((inner_tiles, fields, TC), BF16),
        ],
        scratch_shapes=[
            VMEM((rows, levels, columns), F32),
            VMEM((rows, levels, columns), F32),
            VMEM((per_row, fields * rows, TC), F32),
            VMEM((rows, columns), F32),
        ],
        compiler_params=pltpu.CompilerParams(vmem_limit_bytes=32 * MIB),
        cost_estimate=pl.CostEstimate(flops=10**10, bytes_accessed=20 * MIB, transcendentals=0),
        name="inner",
    )(*[in_hbm(column_state.reshape(levels * rows, columns))] * per_row, force, gain, rate, mixer, export, land_mask)

    outer_final, surface = pl.pallas_call(
        outer_kernel,
        in_specs=[whole] * 8,
        out_specs=[whole] * 2,
        out_shape=[
            jax.ShapeDtypeStruct((2, EDGE, levels, columns), F32),
            jax.ShapeDtypeStruct((tiles, fields, TC), BF16),
        ],
        scratch_shapes=[
            VMEM((2, EDGE + 2, levels, columns), F32),
            VMEM((2, EDGE + 2, levels, columns), F32),
            VMEM((2, 2 * EDGE, columns), F32),
        ],
        compiler_params=pltpu.CompilerParams(vmem_limit_bytes=16 * MIB),
        cost_estimate=pl.CostEstimate(flops=3 * 10**9, bytes_accessed=4 * MIB, transcendentals=0),
        name="outer",
    )(low, high, edges, rate, mixer, export, land_mask, inner_surface)

    new_state = pl.pallas_call(
        write_kernel,
        grid=(per_row,),
        in_specs=[
            pl.BlockSpec((inner_rows, levels, TC), lambda j: (0, 0, j)),
            pl.BlockSpec((2, EDGE, levels, TC), lambda j: (0, 0, 0, j)),
        ],
        out_specs=pl.BlockSpec((levels * rows, TC), lambda j: (0, j)),
        out_shape=jax.ShapeDtypeStruct((levels * rows, columns), F32),
        compiler_params=pltpu.CompilerParams(vmem_limit_bytes=16 * MIB),
        cost_estimate=pl.CostEstimate(flops=0, bytes_accessed=8 * MIB, transcendentals=0),
        name="write",
    )(inner_final, outer_final)

    section_count = lax.axis_size("sec")
    across = [(i, section_count - 1 - i) for i in range(section_count)]
    later = [(i, (i + 2) % count) for i in range(count)]
    earlier = [(i, (i - 2) % count) for i in range(count)]
    mates = [(i, i ^ 1) for i in range(count)]

    core = shard % 2
    wanted = sources.reshape(-1)
    away = wanted // tiles - (shard - core) + 2
    away = away % count
    same_core = away % 2 == core
    positions = (jnp.where(same_core, 0, 3) + away // 2) * tiles + wanted % tiles

    weights = in_hbm(regrid_weights.reshape(tiles, OV * TC, TC))

    here = lax.ppermute(surface, "sec", across)
    here, new_state, positions = lax.optimization_barrier((here, new_state, positions))
    before = lax.ppermute(here, "blk", later)
    after = lax.ppermute(here, "blk", earlier)
    other = lax.ppermute(here, "blk", mates)
    pieces = [before, here, after]
    pieces += [lax.ppermute(before, "blk", mates), other, lax.ppermute(after, "blk", mates)]

    anywhere = pl.BlockSpec(memory_space=pl.ANY)
    coupled = pl.pallas_call(
        regrid_kernel,
        grid_spec=pltpu.PrefetchScalarGridSpec(
            num_scalar_prefetch=1,
            grid=(1,),
            in_specs=[anywhere] * 7,
            out_specs=pl.BlockSpec((fields * rows, columns), lambda i, p: (0, 0)),
            scratch_shapes=[
                VMEM((6 * tiles, fields, TC), BF16),
                VMEM((tiles, OV * TC, TC), BF16),
                VMEM((per_row, fields * rows, TC), F32),
                pltpu.SemaphoreType.DMA((6,)),
                pltpu.SemaphoreType.DMA((16,)),
            ],
        ),
        out_shape=jax.ShapeDtypeStruct((fields * rows, columns), BF16),
        compiler_params=pltpu.CompilerParams(vmem_limit_bytes=24 * MIB),
        cost_estimate=pl.CostEstimate(flops=10**9, bytes_accessed=16 * MIB, transcendentals=0),
        name="regrid",
    )(positions, *pieces, weights)

    return (
        new_state.reshape(1, levels, rows, columns),
        coupled.reshape(1, fields, rows, columns),
    )


def solution(mesh):
    in_specs = (
        P("sec", None, "blk", None),
        P("sec", None, "blk", None),
        P("sec", None, None),
        P("sec", None),
        P("sec", None, None),
        P("sec", None, None),
        P("blk", None),
        P("sec", "blk", None),
        P("sec", "blk", None, None, None),
    )
    out_specs = (P("sec", None, "blk", None), P("sec", None, "blk", None))
    return jax.shard_map(
        on_device, mesh=mesh, in_specs=in_specs, out_specs=out_specs, check_vma=False
    )
```

```python
import jax
import jax.numpy as jnp
from jax import lax
from jax.experimental import pallas as pl
from jax.experimental.pallas import tpu as pltpu
from jax.sharding import PartitionSpec as P

TC = 128
OV = 3
REACH = 2
NSTEP = 4
EDGE = NSTEP
F32 = jnp.float32
BF16 = jnp.bfloat16
VMEM = pltpu.VMEM
MIB = 2**20


def split(value):
    high = value.astype(BF16)
    return high, (value - high.astype(F32)).astype(BF16)


def column(row):
    n = row.shape[1]
    eye = lax.broadcasted_iota(jnp.int32, (n, n), 0) == lax.broadcasted_iota(jnp.int32, (n, n), 1)
    return jnp.sum(jnp.where(eye, jnp.broadcast_to(row, (n, n)), 0.0), axis=1, keepdims=True)


def stacked(matrix):
    high, low = split(matrix)
    return jnp.concatenate([high, high, low], axis=1)


def mixers(mixing, export_map):
    n = mixing.shape[0]
    eye = lax.broadcasted_iota(jnp.int32, (n, n), 0) == lax.broadcasted_iota(jnp.int32, (n, n), 1)
    step = 0.5 * (jnp.where(eye, 1.0, 0.0) + mixing)
    out = jnp.dot(export_map, step, precision=lax.Precision.HIGHEST, preferred_element_type=F32)
    return stacked(jnp.concatenate([step, out], axis=0))


def rows_of(blocks, first, size, stride):
    return jnp.concatenate([block[pl.ds(first, size, stride=stride), :] for block in blocks], axis=1)


def driven(gain, pushed):
    return lax.dot_general(gain, pushed, (((0,), (0,)), ((), ())), preferred_element_type=F32)


def wetness_of(mask):
    return jnp.where((mask > 0) | (lax.axis_index("sec") != 1), 1.0, 0.0)


def blocks_of(ref):
    return [ref.at[index] for index in range(ref.shape[0])]


def diffused(here, above, below, wet, rate, rest):
    columns = here.shape[1]
    rounded = here.astype(BF16)
    left = pltpu.roll(rounded, 1, 1).astype(F32)
    right = pltpu.roll(rounded, columns - 1, 1).astype(F32)
    near = (above + below) + (left + right)
    return jnp.where(wet > 0.0, rate * near + rest * here, here)


def mixed(factor, value):
    high, low = split(value)
    return jnp.dot(factor, jnp.concatenate([high, low, high], axis=0), preferred_element_type=F32)


def load_force(forcing_ref, force):
    value = forcing_ref[...].astype(F32)
    for index in range(force.shape[0]):
        force[index] = value[:, index * TC : (index + 1) * TC]


def edge_kernel(*refs):
    forcing_ref, gain_ref, mask_ref, down_ref, up_ref, force = refs[-6:]
    blocks = (len(refs) - 6) // 2
    top_refs = refs[:blocks]
    bottom_refs = refs[blocks : 2 * blocks]
    fields, levels = gain_ref.shape
    columns = forcing_ref.shape[1]
    rows = forcing_ref.shape[0] // fields
    load_force(forcing_ref, force)
    gain = gain_ref[...]
    for state_refs, out_ref, first, inside in (
        (top_refs, down_ref, 0, 0),
        (bottom_refs, up_ref, rows - EDGE, 8 - EDGE),
    ):
        state = [ref.reshape(levels * 8, TC) for ref in state_refs]
        for row in range(EDGE):
            pushed = rows_of(blocks_of(force), first + row, fields, rows).astype(BF16)
            value = rows_of(state, inside + row, levels, 8) + driven(gain, pushed)
            out_ref[levels * row : levels * (row + 1), :] = value.astype(BF16)
        out_ref[levels * EDGE :, :] = jnp.concatenate(
            [wetness_of(mask_ref[first : first + EDGE, :]), jnp.zeros((16 - EDGE, columns), F32)], axis=0
        ).astype(BF16)


def inner_kernel(
    state_ref,
    forcing_ref,
    gain_ref,
    rate_ref,
    mixing_ref,
    export_ref,
    mask_ref,
    final_ref,
    edge_ref,
    surface_ref,
    even,
    odd,
    arrived,
    force,
    wet_ref,
    sems,
):
    fields, levels = gain_ref.shape
    rows, columns = mask_ref.shape
    blocks = columns // TC

    def arrival(group, block):
        return pltpu.make_async_copy(
            state_ref.at[:, pl.ds(group * 8, 8), pl.ds(block * TC, TC)],
            arrived.at[group, block],
            sems.at[group, block],
        )

    for group in range(rows // 8):
        for block in range(blocks):
            arrival(group, block).start()
    load_force(forcing_ref, force)
    wet_ref[...] = wetness_of(mask_ref[...])
    gain = gain_ref[...]

    @pl.loop(0, rows // 8)
    def _(group):
        for block in range(blocks):
            arrival(group, block).wait()
        state = [arrived.at[group, block].reshape(levels * 8, TC) for block in range(blocks)]
        for part in range(8):
            row = group * 8 + part
            pushed = rows_of(blocks_of(force), row, fields, rows).astype(BF16)
            even[row] = rows_of(state, part, levels, 8) + driven(gain, pushed)

    rate = column(rate_ref[...])
    rest = 1.0 - 4.0 * rate
    factor = mixers(mixing_ref[...], export_ref[...])
    step_factor = factor[:levels]
    for step in range(1, NSTEP + 1):
        source, target = (even, odd) if step % 2 else (odd, even)
        last = step == NSTEP

        todo = rows - 2 * step
        at_once = todo // 2

        @pl.loop(0, todo // at_once)
        def _(group, source=source, target=target, step=step, last=last, at_once=at_once):
            for part in range(at_once):
                row = step + at_once * group + part
                value = diffused(
                    source[row],
                    source[row - 1],
                    source[row + 1],
                    wet_ref[pl.ds(row, 1), :],
                    rate,
                    rest,
                )
                result = mixed(factor if last else step_factor, value)
                if last:
                    final_ref[row - EDGE] = result[:levels]
                    surface = jnp.tanh(result[levels:]).astype(BF16)
                    per_row = columns // TC
                    for tile in range(per_row):
                        surface_ref[(row - EDGE) * per_row + tile] = surface[
                            :, tile * TC : (tile + 1) * TC
                        ]
                else:
                    target[row] = result

    for step in range(NSTEP):
        source = odd if step % 2 else even
        edge_ref[0, step, 0] = source[step]
        edge_ref[0, step, 1] = source[step + 1]
        edge_ref[1, step, 0] = source[rows - 2 - step]
        edge_ref[1, step, 1] = source[rows - 1 - step]


def outer_kernel(
    low_ref,
    high_ref,
    edge_ref,
    rate_ref,
    mixing_ref,
    export_ref,
    mask_ref,
    inner_ref,
    final_ref,
    surface_ref,
    even,
    odd,
    wet,
):
    levels = mixing_ref.shape[0]
    rows, columns = mask_ref.shape
    inner_tiles = inner_ref.shape[0]
    per_row = columns // TC
    rate = column(rate_ref[...])
    rest = 1.0 - 4.0 * rate
    factor = mixers(mixing_ref[...], export_ref[...])
    step_factor = factor[:levels]
    wet[0, 0:EDGE, :] = low_ref[levels * EDGE :, :].astype(F32)[0:EDGE]
    wet[0, EDGE : 2 * EDGE, :] = wetness_of(mask_ref[0:EDGE, :])
    wet[1, 0:EDGE, :] = wetness_of(mask_ref[rows - EDGE : rows, :])
    surface_ref[pl.ds(EDGE * per_row, inner_tiles)] = inner_ref[...]
    wet[1, EDGE : 2 * EDGE, :] = high_ref[levels * EDGE :, :].astype(F32)[0:EDGE]
    for row in range(EDGE):
        even[0, row] = low_ref[levels * row : levels * (row + 1), :].astype(F32)
        even[1, row + 2] = high_ref[levels * row : levels * (row + 1), :].astype(F32)
    for step in range(1, NSTEP + 1):
        source, target = (even, odd) if step % 2 else (odd, even)
        last = step == NSTEP
        for item in range(2):
            source[0, EDGE + item] = edge_ref[0, step - 1, item]
            source[1, item] = edge_ref[1, step - 1, item]
        for side in range(2):
            first_wet = step if side == 0 else NSTEP - step
            shift = 0 if side == 0 else 2
            for row in range(EDGE):
                value = diffused(
                    source[side, row + 1],
                    source[side, row],
                    source[side, row + 2],
                    wet[side, first_wet + row : first_wet + row + 1, :],
                    rate,
                    rest,
                )
                result = mixed(factor if last else step_factor, value)
                if last:
                    final_ref[side, row] = result[:levels]
                    surface = jnp.tanh(result[levels:]).astype(BF16)
                    for tile in range(per_row):
                        surface_ref[(side * (rows - EDGE) + row) * per_row + tile] = surface[
                            :, tile * TC : (tile + 1) * TC
                        ]
                else:
                    target[side, row + shift] = result


def write_kernel(inner_ref, outer_ref, state_ref):
    levels = inner_ref.shape[1]
    rows = inner_ref.shape[0] + 2 * EDGE

    for row in range(EDGE):
        state_ref[pl.ds(row, levels, stride=rows), :] = outer_ref[0, row]
        state_ref[pl.ds(rows - EDGE + row, levels, stride=rows), :] = outer_ref[1, row]

    @pl.loop(0, rows - 2 * EDGE)
    def _(row):
        state_ref[pl.ds(row + EDGE, levels, stride=rows), :] = inner_ref[row]


def regrid_kernel(position_ref, *refs):
    piece_refs = refs[0:6]
    weight_ref, out_ref, held, weights, sums, piece_sems, weight_sems = refs[6:]
    tiles, fields, _ = piece_refs[0].shape
    chunks = weight_sems.shape[0]
    tiles_chunk = tiles // chunks
    per_row, total_rows, _ = sums.shape
    rows = total_rows // fields

    def weight_copy(chunk):
        part = pl.ds(chunk * tiles_chunk, tiles_chunk)
        return pltpu.make_async_copy(weight_ref.at[part], weights.at[part], weight_sems.at[chunk])

    copies = [
        pltpu.make_async_copy(source, held.at[pl.ds(slot * tiles, tiles)], piece_sems.at[slot])
        for slot, source in enumerate(piece_refs)
    ]
    for copy in copies:
        copy.start()
    for chunk in range(chunks):
        weight_copy(chunk).start()
    for copy in copies:
        copy.wait()

    @pl.loop(0, chunks)
    def _(chunk):
        weight_copy(chunk).wait()
        for pair in range(tiles_chunk // 2):
            first = chunk * tiles_chunk + 2 * pair
            lefts = []
            for item in range(2):
                base = (first + item) * OV
                lefts.append(
                    jnp.concatenate([held[position_ref[base + slot]] for slot in range(OV)], axis=1)
                )
            left = jnp.concatenate(lefts, axis=0)
            right = jnp.concatenate([weights[first], weights[first + 1]], axis=1)
            result = jnp.dot(left, right, preferred_element_type=F32)
            for item in range(2):
                tile = 2 * pair + item
                row = chunk * (tiles_chunk // per_row) + tile // per_row
                sums[tile % per_row, pl.ds(row, fields, stride=rows), :] = result[
                    item * fields : (item + 1) * fields, item * TC : (item + 1) * TC
                ]

    for index in range(per_row):
        out_ref[:, index * TC : (index + 1) * TC] = sums[index].astype(BF16)


def in_hbm(value):
    return pltpu.with_memory_space_constraint(value, pltpu.HBM)


def on_device(
    column_state,
    forcing,
    couple_gain,
    diffusion,
    mixing,
    export_map,
    land_mask,
    sources,
    regrid_weights,
):
    shard = lax.axis_index("blk")
    count = lax.axis_size("blk")
    _, levels, rows, columns = column_state.shape
    fields = forcing.shape[1]
    tiles = rows * columns // TC
    per_row = columns // TC
    inner_rows = rows - 2 * EDGE
    inner_tiles = inner_rows * per_row
    state = in_hbm(column_state[0])
    force = in_hbm(forcing.reshape(fields * rows, columns))
    gain = in_hbm(couple_gain[0].T)
    land_mask = in_hbm(land_mask)
    rate = diffusion
    mixer = mixing[0]
    export = export_map[0]
    whole = pl.BlockSpec(memory_space=VMEM)

    payload = levels * EDGE + 16
    down, up = pl.pallas_call(
        edge_kernel,
        grid=(1,),
        in_specs=[
            pl.BlockSpec((levels, 8, TC), lambda i, j=index, k=k: (0, k, j))
            for k in (0, rows // 8 - 1)
            for index in range(per_row)
        ]
        + [
            pl.BlockSpec((fields * rows, columns), lambda i: (0, 0)),
            pl.BlockSpec((fields, levels), lambda i: (0, 0)),
            pl.BlockSpec((rows, columns), lambda i: (0, 0)),
        ],
        out_specs=[pl.BlockSpec((payload, columns), lambda i: (0, 0))] * 2,
        out_shape=[jax.ShapeDtypeStruct((payload, columns), BF16)] * 2,
        scratch_shapes=[VMEM((per_row, fields * rows, TC), F32)],
        compiler_params=pltpu.CompilerParams(vmem_limit_bytes=16 * MIB),
        cost_estimate=pl.CostEstimate(flops=10**7, bytes_accessed=3 * MIB, transcendentals=0),
        name="edges",
    )(*[state] * (2 * per_row), force, gain, land_mask)
    upward = [(i, i + 1) for i in range(count - 1)]
    downward = [(i + 1, i) for i in range(count - 1)]
    low = lax.ppermute(up, "blk", upward)
    high = lax.ppermute(down, "blk", downward)

    inner_final, edges, inner_surface = pl.pallas_call(
        inner_kernel,
        in_specs=[pl.BlockSpec(memory_space=pl.ANY)] + [whole] * 6,
        out_specs=[whole] * 3,
        out_shape=[
            jax.ShapeDtypeStruct((inner_rows, levels, columns), F32),
            jax.ShapeDtypeStruct((2, NSTEP, 2, levels, columns), F32),
            jax.ShapeDtypeStruct((inner_tiles, fields, TC), BF16),
        ],
        scratch_shapes=[
            VMEM((rows, levels, columns), F32),
            VMEM((rows, levels, columns), F32),
            VMEM((rows // 8, per_row, levels, 8, TC), F32),
            VMEM((per_row, fields * rows, TC), F32),
            VMEM((rows, columns), F32),
            pltpu.SemaphoreType.DMA((rows // 8, per_row)),
        ],
        compiler_params=pltpu.CompilerParams(vmem_limit_bytes=32 * MIB),
        cost_estimate=pl.CostEstimate(flops=10**10, bytes_accessed=20 * MIB, transcendentals=0),
        name="inner",
    )(state, force, gain, rate, mixer, export, land_mask)

    outer_final, surface = pl.pallas_call(
        outer_kernel,
        in_specs=[whole] * 8,
        out_specs=[whole] * 2,
        out_shape=[
            jax.ShapeDtypeStruct((2, EDGE, levels, columns), F32),
            jax.ShapeDtypeStruct((tiles, fields, TC), BF16),
        ],
        scratch_shapes=[
            VMEM((2, EDGE + 2, levels, columns), F32),
            VMEM((2, EDGE + 2, levels, columns), F32),
            VMEM((2, 2 * EDGE, columns), F32),
        ],
        compiler_params=pltpu.CompilerParams(vmem_limit_bytes=16 * MIB),
        cost_estimate=pl.CostEstimate(flops=3 * 10**9, bytes_accessed=4 * MIB, transcendentals=0),
        name="outer",
    )(low, high, edges, rate, mixer, export, land_mask, inner_surface)

    new_state = pl.pallas_call(
        write_kernel,
        grid=(per_row,),
        in_specs=[
            pl.BlockSpec((inner_rows, levels, TC), lambda j: (0, 0, j)),
            pl.BlockSpec((2, EDGE, levels, TC), lambda j: (0, 0, 0, j)),
        ],
        out_specs=pl.BlockSpec((levels * rows, TC), lambda j: (0, j)),
        out_shape=jax.ShapeDtypeStruct((levels * rows, columns), F32),
        compiler_params=pltpu.CompilerParams(vmem_limit_bytes=16 * MIB),
        cost_estimate=pl.CostEstimate(flops=0, bytes_accessed=8 * MIB, transcendentals=0),
        name="write",
    )(inner_final, outer_final)

    section_count = lax.axis_size("sec")
    across = [(i, section_count - 1 - i) for i in range(section_count)]
    later = [(i, (i + 2) % count) for i in range(count)]
    earlier = [(i, (i - 2) % count) for i in range(count)]
    mates = [(i, i ^ 1) for i in range(count)]

    core = shard % 2
    wanted = sources.reshape(-1)
    away = wanted // tiles - (shard - core) + 2
    away = away % count
    same_core = away % 2 == core
    positions = (jnp.where(same_core, 0, 3) + away // 2) * tiles + wanted % tiles

    weights = in_hbm(regrid_weights.reshape(tiles, OV * TC, TC))

    here = lax.ppermute(surface, "sec", across)
    here, new_state, positions = lax.optimization_barrier((here, new_state, positions))
    before = lax.ppermute(here, "blk", later)
    after = lax.ppermute(here, "blk", earlier)
    other = lax.ppermute(here, "blk", mates)
    pieces = [before, here, after]
    pieces += [lax.ppermute(before, "blk", mates), other, lax.ppermute(after, "blk", mates)]

    anywhere = pl.BlockSpec(memory_space=pl.ANY)
    coupled = pl.pallas_call(
        regrid_kernel,
        grid_spec=pltpu.PrefetchScalarGridSpec(
            num_scalar_prefetch=1,
            grid=(1,),
            in_specs=[anywhere] * 7,
            out_specs=pl.BlockSpec((fields * rows, columns), lambda i, p: (0, 0)),
            scratch_shapes=[
                VMEM((6 * tiles, fields, TC), BF16),
                VMEM((tiles, OV * TC, TC), BF16),
                VMEM((per_row, fields * rows, TC), F32),
                pltpu.SemaphoreType.DMA((6,)),
                pltpu.SemaphoreType.DMA((16,)),
            ],
        ),
        out_shape=jax.ShapeDtypeStruct((fields * rows, columns), BF16),
        compiler_params=pltpu.CompilerParams(vmem_limit_bytes=24 * MIB),
        cost_estimate=pl.CostEstimate(flops=10**9, bytes_accessed=16 * MIB, transcendentals=0),
        name="regrid",
    )(positions, *pieces, weights)

    return (
        new_state.reshape(1, levels, rows, columns),
        coupled.reshape(1, fields, rows, columns),
    )


def solution(mesh):
    in_specs = (
        P("sec", None, "blk", None),
        P("sec", None, "blk", None),
        P("sec", None, None),
        P("sec", None),
        P("sec", None, None),
        P("sec", None, None),
        P("blk", None),
        P("sec", "blk", None),
        P("sec", "blk", None, None, None),
    )
    out_specs = (P("sec", None, "blk", None), P("sec", None, "blk", None))
    return jax.shard_map(
        on_device, mesh=mesh, in_specs=in_specs, out_specs=out_specs, check_vma=False
    )
```

```python
import jax
import jax.numpy as jnp
from jax import lax
from jax.experimental import pallas as pl
from jax.experimental.pallas import tpu as pltpu
from jax.sharding import PartitionSpec as P

TC = 128
OV = 3
REACH = 2
NSTEP = 4
EDGE = NSTEP
F32 = jnp.float32
BF16 = jnp.bfloat16
VMEM = pltpu.VMEM
MIB = 2**20


def split(value):
    high = value.astype(BF16)
    return high, (value - high.astype(F32)).astype(BF16)


def column(row):
    n = row.shape[1]
    eye = lax.broadcasted_iota(jnp.int32, (n, n), 0) == lax.broadcasted_iota(jnp.int32, (n, n), 1)
    return jnp.sum(jnp.where(eye, jnp.broadcast_to(row, (n, n)), 0.0), axis=1, keepdims=True)


def stacked(matrix):
    high, low = split(matrix)
    return jnp.concatenate([high, high, low], axis=1)


def mixers(mixing, export_map):
    n = mixing.shape[0]
    eye = lax.broadcasted_iota(jnp.int32, (n, n), 0) == lax.broadcasted_iota(jnp.int32, (n, n), 1)
    step = 0.5 * (jnp.where(eye, 1.0, 0.0) + mixing)
    out = jnp.dot(export_map, step, precision=lax.Precision.HIGHEST, preferred_element_type=F32)
    return stacked(jnp.concatenate([step, out], axis=0))


def rows_of(blocks, first, size, stride):
    return jnp.concatenate([block[pl.ds(first, size, stride=stride), :] for block in blocks], axis=1)


def driven(gain, pushed):
    return lax.dot_general(gain, pushed, (((0,), (0,)), ((), ())), preferred_element_type=F32)


def wetness_of(mask):
    return jnp.where((mask > 0) | (lax.axis_index("sec") != 1), 1.0, 0.0)


def blocks_of(ref):
    return [ref.at[index] for index in range(ref.shape[0])]


def diffused(here, above, below, wet, rate, rest):
    columns = here.shape[1]
    rounded = here.astype(BF16)
    left = pltpu.roll(rounded, 1, 1).astype(F32)
    right = pltpu.roll(rounded, columns - 1, 1).astype(F32)
    near = (above + below) + (left + right)
    return jnp.where(wet > 0.0, rate * near + rest * here, here)


def mixed(factor, value):
    high, low = split(value)
    return jnp.dot(factor, jnp.concatenate([high, low, high], axis=0), preferred_element_type=F32)


def load_force(forcing_ref, force):
    value = forcing_ref[...].astype(F32)
    for index in range(force.shape[0]):
        force[index] = value[:, index * TC : (index + 1) * TC]


def edge_kernel(*refs):
    forcing_ref, gain_ref, mask_ref, down_ref, up_ref, force = refs[-6:]
    blocks = (len(refs) - 6) // 2
    top_refs = refs[:blocks]
    bottom_refs = refs[blocks : 2 * blocks]
    fields, levels = gain_ref.shape
    columns = forcing_ref.shape[1]
    rows = forcing_ref.shape[0] // fields
    load_force(forcing_ref, force)
    gain = gain_ref[...]
    for state_refs, out_ref, first, inside in (
        (top_refs, down_ref, 0, 0),
        (bottom_refs, up_ref, rows - EDGE, 8 - EDGE),
    ):
        state = [ref.reshape(levels * 8, TC) for ref in state_refs]
        for row in range(EDGE):
            pushed = rows_of(blocks_of(force), first + row, fields, rows).astype(BF16)
            value = rows_of(state, inside + row, levels, 8) + driven(gain, pushed)
            out_ref[levels * row : levels * (row + 1), :] = value.astype(BF16)
        out_ref[levels * EDGE :, :] = jnp.concatenate(
            [wetness_of(mask_ref[first : first + EDGE, :]), jnp.zeros((16 - EDGE, columns), F32)], axis=0
        ).astype(BF16)


def inner_kernel(
    state_ref,
    forcing_ref,
    gain_ref,
    rate_ref,
    mixing_ref,
    export_ref,
    mask_ref,
    final_ref,
    edge_ref,
    surface_ref,
    even,
    odd,
    arrived,
    force,
    wet_ref,
    sems,
):
    fields, levels = gain_ref.shape
    rows, columns = mask_ref.shape
    blocks = columns // TC

    def arrival(group, block):
        return pltpu.make_async_copy(
            state_ref.at[:, pl.ds(group * 8, 8), pl.ds(block * TC, TC)],
            arrived.at[group, block],
            sems.at[group, block],
        )

    for group in range(rows // 8):
        for block in range(blocks):
            arrival(group, block).start()
    load_force(forcing_ref, force)
    wet_ref[...] = wetness_of(mask_ref[...])
    gain = gain_ref[...]
    rate = column(rate_ref[...])
    rest = 1.0 - 4.0 * rate
    factor = mixers(mixing_ref[...], export_ref[...])
    step_factor = factor[:levels]

    @pl.loop(0, rows // 8)
    def _(group):
        for block in range(blocks):
            arrival(group, block).wait()
        state = [arrived.at[group, block].reshape(levels * 8, TC) for block in range(blocks)]
        for part in range(8):
            row = group * 8 + part
            pushed = rows_of(blocks_of(force), row, fields, rows).astype(BF16)
            even[row] = rows_of(state, part, levels, 8) + driven(gain, pushed)

    for step in range(1, NSTEP + 1):
        source, target = (even, odd) if step % 2 else (odd, even)
        last = step == NSTEP

        todo = rows - 2 * step
        at_once = todo // 2

        @pl.loop(0, todo // at_once)
        def _(group, source=source, target=target, step=step, last=last, at_once=at_once):
            for part in range(at_once):
                row = step + at_once * group + part
                value = diffused(
                    source[row],
                    source[row - 1],
                    source[row + 1],
                    wet_ref[pl.ds(row, 1), :],
                    rate,
                    rest,
                )
                result = mixed(factor if last else step_factor, value)
                if last:
                    final_ref[row - EDGE] = result[:levels]
                    surface = jnp.tanh(result[levels:]).astype(BF16)
                    per_row = columns // TC
                    for tile in range(per_row):
                        surface_ref[(row - EDGE) * per_row + tile] = surface[
                            :, tile * TC : (tile + 1) * TC
                        ]
                else:
                    target[row] = result

    for step in range(NSTEP):
        source = odd if step % 2 else even
        edge_ref[0, step, 0] = source[step]
        edge_ref[0, step, 1] = source[step + 1]
        edge_ref[1, step, 0] = source[rows - 2 - step]
        edge_ref[1, step, 1] = source[rows - 1 - step]


def outer_kernel(
    low_ref,
    high_ref,
    edge_ref,
    rate_ref,
    mixing_ref,
    export_ref,
    mask_ref,
    inner_ref,
    final_ref,
    surface_ref,
    even,
    odd,
    wet,
):
    levels = mixing_ref.shape[0]
    rows, columns = mask_ref.shape
    inner_tiles = inner_ref.shape[0]
    per_row = columns // TC
    rate = column(rate_ref[...])
    rest = 1.0 - 4.0 * rate
    factor = mixers(mixing_ref[...], export_ref[...])
    step_factor = factor[:levels]
    wet[0, 0:EDGE, :] = low_ref[levels * EDGE :, :].astype(F32)[0:EDGE]
    wet[0, EDGE : 2 * EDGE, :] = wetness_of(mask_ref[0:EDGE, :])
    wet[1, 0:EDGE, :] = wetness_of(mask_ref[rows - EDGE : rows, :])
    surface_ref[pl.ds(EDGE * per_row, inner_tiles)] = inner_ref[...]
    wet[1, EDGE : 2 * EDGE, :] = high_ref[levels * EDGE :, :].astype(F32)[0:EDGE]
    for row in range(EDGE):
        even[0, row] = low_ref[levels * row : levels * (row + 1), :].astype(F32)
        even[1, row + 2] = high_ref[levels * row : levels * (row + 1), :].astype(F32)
    for step in range(1, NSTEP + 1):
        source, target = (even, odd) if step % 2 else (odd, even)
        last = step == NSTEP
        for item in range(2):
            source[0, EDGE + item] = edge_ref[0, step - 1, item]
            source[1, item] = edge_ref[1, step - 1, item]
        for side in range(2):
            first_wet = step if side == 0 else NSTEP - step
            shift = 0 if side == 0 else 2
            for row in range(EDGE):
                value = diffused(
                    source[side, row + 1],
                    source[side, row],
                    source[side, row + 2],
                    wet[side, first_wet + row : first_wet + row + 1, :],
                    rate,
                    rest,
                )
                result = mixed(factor if last else step_factor, value)
                if last:
                    final_ref[side, row] = result[:levels]
                    surface = jnp.tanh(result[levels:]).astype(BF16)
                    for tile in range(per_row):
                        surface_ref[(side * (rows - EDGE) + row) * per_row + tile] = surface[
                            :, tile * TC : (tile + 1) * TC
                        ]
                else:
                    target[side, row + shift] = result


def write_kernel(inner_ref, outer_ref, state_ref):
    levels = inner_ref.shape[1]
    rows = inner_ref.shape[0] + 2 * EDGE

    for row in range(EDGE):
        state_ref[pl.ds(row, levels, stride=rows), :] = outer_ref[0, row]
        state_ref[pl.ds(rows - EDGE + row, levels, stride=rows), :] = outer_ref[1, row]

    @pl.loop(0, rows - 2 * EDGE)
    def _(row):
        state_ref[pl.ds(row + EDGE, levels, stride=rows), :] = inner_ref[row]


def load_kernel(source_ref, target_ref, sems):
    chunks = sems.shape[0]
    size = source_ref.shape[0] // chunks
    copies = [
        pltpu.make_async_copy(
            source_ref.at[pl.ds(chunk * size, size)],
            target_ref.at[pl.ds(chunk * size, size)],
            sems.at[chunk],
        )
        for chunk in range(chunks)
    ]
    for copy in copies:
        copy.start()
    for copy in copies:
        copy.wait()


def regrid_kernel(position_ref, *refs):
    piece_refs = refs[0:6]
    weights, out_ref, held, sums, sems = refs[6:]
    tiles, fields, _ = piece_refs[0].shape
    chunks = 4
    tiles_chunk = tiles // chunks
    per_row, total_rows, _ = sums.shape
    rows = total_rows // fields
    copies = [
        pltpu.make_async_copy(source, held.at[pl.ds(index * tiles, tiles)], sems.at[index])
        for index, source in enumerate(piece_refs)
    ]
    for copy in copies:
        copy.start()
    for copy in copies:
        copy.wait()

    @pl.loop(0, chunks)
    def _(chunk):
        for pair in range(tiles_chunk // 2):
            first = chunk * tiles_chunk + 2 * pair
            lefts = []
            for item in range(2):
                base = (first + item) * OV
                lefts.append(
                    jnp.concatenate([held[position_ref[base + slot]] for slot in range(OV)], axis=1)
                )
            left = jnp.concatenate(lefts, axis=0)
            right = jnp.concatenate([weights[first], weights[first + 1]], axis=1)
            result = jnp.dot(left, right, preferred_element_type=F32)
            for item in range(2):
                tile = 2 * pair + item
                row = chunk * (tiles_chunk // per_row) + tile // per_row
                sums[tile % per_row, pl.ds(row, fields, stride=rows), :] = result[
                    item * fields : (item + 1) * fields, item * TC : (item + 1) * TC
                ]

    for index in range(per_row):
        out_ref[:, index * TC : (index + 1) * TC] = sums[index].astype(BF16)


def in_hbm(value):
    return pltpu.with_memory_space_constraint(value, pltpu.HBM)


def on_device(
    column_state,
    forcing,
    couple_gain,
    diffusion,
    mixing,
    export_map,
    land_mask,
    sources,
    regrid_weights,
):
    shard = lax.axis_index("blk")
    count = lax.axis_size("blk")
    _, levels, rows, columns = column_state.shape
    fields = forcing.shape[1]
    tiles = rows * columns // TC
    per_row = columns // TC
    inner_rows = rows - 2 * EDGE
    inner_tiles = inner_rows * per_row
    state = in_hbm(column_state[0])
    force = in_hbm(forcing.reshape(fields * rows, columns))
    gain = in_hbm(couple_gain[0].T)
    land_mask = in_hbm(land_mask)
    rate = diffusion
    mixer = mixing[0]
    export = export_map[0]
    whole = pl.BlockSpec(memory_space=VMEM)
    anywhere = pl.BlockSpec(memory_space=pl.ANY)

    payload = levels * EDGE + 16
    down, up = pl.pallas_call(
        edge_kernel,
        grid=(1,),
        in_specs=[
            pl.BlockSpec((levels, 8, TC), lambda i, j=index, k=k: (0, k, j))
            for k in (0, rows // 8 - 1)
            for index in range(per_row)
        ]
        + [
            pl.BlockSpec((fields * rows, columns), lambda i: (0, 0)),
            pl.BlockSpec((fields, levels), lambda i: (0, 0)),
            pl.BlockSpec((rows, columns), lambda i: (0, 0)),
        ],
        out_specs=[pl.BlockSpec((payload, columns), lambda i: (0, 0))] * 2,
        out_shape=[jax.ShapeDtypeStruct((payload, columns), BF16)] * 2,
        scratch_shapes=[VMEM((per_row, fields * rows, TC), F32)],
        compiler_params=pltpu.CompilerParams(vmem_limit_bytes=16 * MIB),
        cost_estimate=pl.CostEstimate(flops=10**7, bytes_accessed=3 * MIB, transcendentals=0),
        name="edges",
    )(*[state] * (2 * per_row), force, gain, land_mask)
    upward = [(i, i + 1) for i in range(count - 1)]
    downward = [(i + 1, i) for i in range(count - 1)]
    low = lax.ppermute(up, "blk", upward)
    high = lax.ppermute(down, "blk", downward)

    inner_final, edges, inner_surface = pl.pallas_call(
        inner_kernel,
        in_specs=[pl.BlockSpec(memory_space=pl.ANY)] + [whole] * 6,
        out_specs=[whole] * 3,
        out_shape=[
            VMEM((inner_rows, levels, columns), F32),
            VMEM((2, NSTEP, 2, levels, columns), F32),
            VMEM((inner_tiles, fields, TC), BF16),
        ],
        scratch_shapes=[
            VMEM((rows, levels, columns), F32),
            VMEM((rows, levels, columns), F32),
            VMEM((rows // 8, per_row, levels, 8, TC), F32),
            VMEM((per_row, fields * rows, TC), F32),
            VMEM((rows, columns), F32),
            pltpu.SemaphoreType.DMA((rows // 8, per_row)),
        ],
        compiler_params=pltpu.CompilerParams(vmem_limit_bytes=18 * MIB),
        cost_estimate=pl.CostEstimate(flops=10**10, bytes_accessed=20 * MIB, transcendentals=0),
        name="inner",
    )(state, force, gain, rate, mixer, export, land_mask)

    outer_final, surface = pl.pallas_call(
        outer_kernel,
        in_specs=[whole] * 8,
        out_specs=[whole] * 2,
        out_shape=[
            VMEM((2, EDGE, levels, columns), F32),
            VMEM((tiles, fields, TC), BF16),
        ],
        scratch_shapes=[
            VMEM((2, EDGE + 2, levels, columns), F32),
            VMEM((2, EDGE + 2, levels, columns), F32),
            VMEM((2, 2 * EDGE, columns), F32),
        ],
        compiler_params=pltpu.CompilerParams(vmem_limit_bytes=16 * MIB),
        cost_estimate=pl.CostEstimate(flops=3 * 10**9, bytes_accessed=4 * MIB, transcendentals=0),
        name="outer",
    )(low, high, edges, rate, mixer, export, land_mask, inner_surface)

    section_count = lax.axis_size("sec")
    across = [(i, section_count - 1 - i) for i in range(section_count)]
    later = [(i, (i + 2) % count) for i in range(count)]
    earlier = [(i, (i - 2) % count) for i in range(count)]
    mates = [(i, i ^ 1) for i in range(count)]

    core = shard % 2
    wanted = sources.reshape(-1)
    away = wanted // tiles - (shard - core) + 2
    away = away % count
    same_core = away % 2 == core
    positions = (jnp.where(same_core, 0, 3) + away // 2) * tiles + wanted % tiles

    weights = in_hbm(regrid_weights.reshape(tiles, OV * TC, TC))

    raw = regrid_weights.reshape(tiles, OV * TC, TC)
    raw, surface = lax.optimization_barrier((raw, surface))
    here = lax.ppermute(surface, "sec", across)
    weights = pl.pallas_call(
        load_kernel,
        in_specs=[anywhere],
        out_specs=whole,
        out_shape=VMEM((tiles, OV * TC, TC), BF16),
        scratch_shapes=[pltpu.SemaphoreType.DMA((16,))],
        compiler_params=pltpu.CompilerParams(vmem_limit_bytes=16 * MIB),
        cost_estimate=pl.CostEstimate(flops=0, bytes_accessed=12 * MIB, transcendentals=0),
        name="load",
    )(in_hbm(raw))
    here, positions, inner_final, outer_final, weights = lax.optimization_barrier(
        (here, positions, inner_final, outer_final, weights)
    )
    before = lax.ppermute(here, "blk", later)
    after = lax.ppermute(here, "blk", earlier)
    other = lax.ppermute(here, "blk", mates)
    new_state = pl.pallas_call(
        write_kernel,
        grid=(per_row,),
        in_specs=[
            pl.BlockSpec((inner_rows, levels, TC), lambda j: (0, 0, j)),
            pl.BlockSpec((2, EDGE, levels, TC), lambda j: (0, 0, 0, j)),
        ],
        out_specs=pl.BlockSpec((levels * rows, TC), lambda j: (0, j)),
        out_shape=jax.ShapeDtypeStruct((levels * rows, columns), F32),
        compiler_params=pltpu.CompilerParams(vmem_limit_bytes=8 * MIB),
        cost_estimate=pl.CostEstimate(flops=0, bytes_accessed=8 * MIB, transcendentals=0),
        name="write",
    )(inner_final, outer_final)
    before, after, other, new_state = lax.optimization_barrier((before, after, other, new_state))
    pieces = [before, here, after]
    pieces += [lax.ppermute(before, "blk", mates), other, lax.ppermute(after, "blk", mates)]

    coupled = pl.pallas_call(
        regrid_kernel,
        grid_spec=pltpu.PrefetchScalarGridSpec(
            num_scalar_prefetch=1,
            grid=(1,),
            in_specs=[anywhere] * 6 + [whole],
            out_specs=pl.BlockSpec((fields * rows, columns), lambda i, p: (0, 0)),
            scratch_shapes=[
                VMEM((6 * tiles, fields, TC), BF16),
                VMEM((per_row, fields * rows, TC), F32),
                pltpu.SemaphoreType.DMA((6,)),
            ],
        ),
        out_shape=jax.ShapeDtypeStruct((fields * rows, columns), BF16),
        compiler_params=pltpu.CompilerParams(vmem_limit_bytes=8 * MIB),
        cost_estimate=pl.CostEstimate(flops=10**9, bytes_accessed=16 * MIB, transcendentals=0),
        name="regrid",
    )(positions, *pieces, weights)

    return (
        new_state.reshape(1, levels, rows, columns),
        coupled.reshape(1, fields, rows, columns),
    )


def solution(mesh):
    in_specs = (
        P("sec", None, "blk", None),
        P("sec", None, "blk", None),
        P("sec", None, None),
        P("sec", None),
        P("sec", None, None),
        P("sec", None, None),
        P("blk", None),
        P("sec", "blk", None),
        P("sec", "blk", None, None, None),
    )
    out_specs = (P("sec", None, "blk", None), P("sec", None, "blk", None))
    return jax.shard_map(
        on_device, mesh=mesh, in_specs=in_specs, out_specs=out_specs, check_vma=False
    )
```

```python
import jax
import jax.numpy as jnp
from jax import lax
from jax.experimental import pallas as pl
from jax.experimental.pallas import tpu as pltpu
from jax.sharding import PartitionSpec as P

TC = 128
OV = 3
REACH = 2
NSTEP = 4
EDGE = NSTEP
F32 = jnp.float32
BF16 = jnp.bfloat16
VMEM = pltpu.VMEM
MIB = 2**20


def split(value):
    high = value.astype(BF16)
    return high, (value - high.astype(F32)).astype(BF16)


def column(row):
    n = row.shape[1]
    eye = lax.broadcasted_iota(jnp.int32, (n, n), 0) == lax.broadcasted_iota(jnp.int32, (n, n), 1)
    return jnp.sum(jnp.where(eye, jnp.broadcast_to(row, (n, n)), 0.0), axis=1, keepdims=True)


def stacked(matrix):
    high, low = split(matrix)
    return jnp.concatenate([high, high, low], axis=1)


def mixers(mixing, export_map):
    n = mixing.shape[0]
    eye = lax.broadcasted_iota(jnp.int32, (n, n), 0) == lax.broadcasted_iota(jnp.int32, (n, n), 1)
    step = 0.5 * (jnp.where(eye, 1.0, 0.0) + mixing)
    out = jnp.dot(export_map, step, precision=lax.Precision.HIGHEST, preferred_element_type=F32)
    return stacked(jnp.concatenate([step, out], axis=0))


def rows_of(blocks, first, size, stride):
    return jnp.concatenate([block[pl.ds(first, size, stride=stride), :] for block in blocks], axis=1)


def driven(gain, pushed):
    return lax.dot_general(gain, pushed, (((0,), (0,)), ((), ())), preferred_element_type=F32)


def wetness_of(mask):
    return jnp.where((mask > 0) | (lax.axis_index("sec") != 1), 1.0, 0.0)


def blocks_of(ref):
    return [ref.at[index] for index in range(ref.shape[0])]


def diffused(here, above, below, wet, rate):
    columns = here.shape[1]
    rounded = here.astype(BF16)
    left = pltpu.roll(rounded, 1, 1).astype(F32)
    right = pltpu.roll(rounded, columns - 1, 1).astype(F32)
    near = (above + below) + (left + right)
    return here + wet * (rate * (near - 4.0 * here))


def mixed(factor, value):
    high, low = split(value)
    return jnp.dot(factor, jnp.concatenate([high, low, high], axis=0), preferred_element_type=F32)


def load_force(forcing_ref, force):
    value = forcing_ref[...].astype(F32)
    for index in range(force.shape[0]):
        force[index] = value[:, index * TC : (index + 1) * TC]


def edge_kernel(*refs):
    forcing_ref, gain_ref, mask_ref, down_ref, up_ref, force = refs[-6:]
    blocks = (len(refs) - 6) // 2
    top_refs = refs[:blocks]
    bottom_refs = refs[blocks : 2 * blocks]
    fields, levels = gain_ref.shape
    columns = forcing_ref.shape[1]
    rows = forcing_ref.shape[0] // fields
    load_force(forcing_ref, force)
    gain = gain_ref[...]
    for state_refs, out_ref, first, inside in (
        (top_refs, down_ref, 0, 0),
        (bottom_refs, up_ref, rows - EDGE, 8 - EDGE),
    ):
        state = [ref.reshape(levels * 8, TC) for ref in state_refs]
        for row in range(EDGE):
            pushed = rows_of(blocks_of(force), first + row, fields, rows).astype(BF16)
            value = rows_of(state, inside + row, levels, 8) + driven(gain, pushed)
            out_ref[levels * row : levels * (row + 1), :] = value.astype(BF16)
        out_ref[levels * EDGE :, :] = jnp.concatenate(
            [wetness_of(mask_ref[first : first + EDGE, :]), jnp.zeros((16 - EDGE, columns), F32)], axis=0
        ).astype(BF16)


def inner_kernel(
    state_ref,
    forcing_ref,
    gain_ref,
    rate_ref,
    mixing_ref,
    export_ref,
    mask_ref,
    final_ref,
    edge_ref,
    surface_ref,
    even,
    odd,
    arrived,
    force,
    wet_ref,
    sems,
):
    fields, levels = gain_ref.shape
    rows, columns = mask_ref.shape
    blocks = columns // TC

    def arrival(group, block):
        return pltpu.make_async_copy(
            state_ref.at[:, pl.ds(group * 8, 8), pl.ds(block * TC, TC)],
            arrived.at[group, block],
            sems.at[group, block],
        )

    for group in range(rows // 8):
        for block in range(blocks):
            arrival(group, block).start()
    load_force(forcing_ref, force)
    wet_ref[...] = wetness_of(mask_ref[...])
    gain = gain_ref[...]
    rate = column(rate_ref[...])
    factor = mixers(mixing_ref[...], export_ref[...])
    step_factor = factor[:levels]

    for group in range(rows // 8):
        for block in range(blocks):
            arrival(group, block).wait()
        state = [arrived.at[group, block].reshape(levels * 8, TC) for block in range(blocks)]
        for part in range(8):
            row = group * 8 + part
            pushed = rows_of(blocks_of(force), row, fields, rows).astype(BF16)
            even[row] = rows_of(state, part, levels, 8) + driven(gain, pushed)

    for step in range(1, NSTEP + 1):
        source, target = (even, odd) if step % 2 else (odd, even)
        last = step == NSTEP


        for row in range(step, rows - step):
            value = diffused(
                source[row],
                source[row - 1],
                source[row + 1],
                wet_ref[row : row + 1, :],
                rate,
            )
            result = mixed(factor if last else step_factor, value)
            if last:
                final_ref[row - EDGE] = result[:levels]
                surface = jnp.tanh(result[levels:]).astype(BF16)
                per_row = columns // TC
                for tile in range(per_row):
                    surface_ref[(row - EDGE) * per_row + tile] = surface[
                        :, tile * TC : (tile + 1) * TC
                    ]
            else:
                target[row] = result

    for step in range(NSTEP):
        source = odd if step % 2 else even
        edge_ref[0, step, 0] = source[step]
        edge_ref[0, step, 1] = source[step + 1]
        edge_ref[1, step, 0] = source[rows - 2 - step]
        edge_ref[1, step, 1] = source[rows - 1 - step]


def outer_kernel(
    low_ref,
    high_ref,
    edge_ref,
    rate_ref,
    mixing_ref,
    export_ref,
    mask_ref,
    inner_ref,
    final_ref,
    surface_ref,
    even,
    odd,
    wet,
):
    levels = mixing_ref.shape[0]
    rows, columns = mask_ref.shape
    inner_tiles = inner_ref.shape[0]
    per_row = columns // TC
    rate = column(rate_ref[...])
    factor = mixers(mixing_ref[...], export_ref[...])
    step_factor = factor[:levels]
    wet[0, 0:EDGE, :] = low_ref[levels * EDGE :, :].astype(F32)[0:EDGE]
    wet[0, EDGE : 2 * EDGE, :] = wetness_of(mask_ref[0:EDGE, :])
    wet[1, 0:EDGE, :] = wetness_of(mask_ref[rows - EDGE : rows, :])
    surface_ref[pl.ds(EDGE * per_row, inner_tiles)] = inner_ref[...]
    wet[1, EDGE : 2 * EDGE, :] = high_ref[levels * EDGE :, :].astype(F32)[0:EDGE]
    for row in range(EDGE):
        even[0, row] = low_ref[levels * row : levels * (row + 1), :].astype(F32)
        even[1, row + 2] = high_ref[levels * row : levels * (row + 1), :].astype(F32)
    for step in range(1, NSTEP + 1):
        source, target = (even, odd) if step % 2 else (odd, even)
        last = step == NSTEP
        for item in range(2):
            source[0, EDGE + item] = edge_ref[0, step - 1, item]
            source[1, item] = edge_ref[1, step - 1, item]
        for side in range(2):
            first_wet = step if side == 0 else NSTEP - step
            shift = 0 if side == 0 else 2
            for row in range(EDGE):
                value = diffused(
                    source[side, row + 1],
                    source[side, row],
                    source[side, row + 2],
                    wet[side, first_wet + row : first_wet + row + 1, :],
                    rate,
                )
                result = mixed(factor if last else step_factor, value)
                if last:
                    final_ref[side, row] = result[:levels]
                    surface = jnp.tanh(result[levels:]).astype(BF16)
                    for tile in range(per_row):
                        surface_ref[(side * (rows - EDGE) + row) * per_row + tile] = surface[
                            :, tile * TC : (tile + 1) * TC
                        ]
                else:
                    target[side, row + shift] = result


def write_kernel(inner_ref, outer_ref, state_ref):
    levels = inner_ref.shape[1]
    rows = inner_ref.shape[0] + 2 * EDGE

    for row in range(EDGE):
        state_ref[pl.ds(row, levels, stride=rows), :] = outer_ref[0, row]
        state_ref[pl.ds(rows - EDGE + row, levels, stride=rows), :] = outer_ref[1, row]

    @pl.loop(0, rows - 2 * EDGE)
    def _(row):
        state_ref[pl.ds(row + EDGE, levels, stride=rows), :] = inner_ref[row]


def load_kernel(source_ref, target_ref, sems):
    chunks = sems.shape[0]
    size = source_ref.shape[0] // chunks
    copies = [
        pltpu.make_async_copy(
            source_ref.at[pl.ds(chunk * size, size)],
            target_ref.at[pl.ds(chunk * size, size)],
            sems.at[chunk],
        )
        for chunk in range(chunks)
    ]
    for copy in copies:
        copy.start()
    for copy in copies:
        copy.wait()


def regrid_kernel(position_ref, *refs):
    piece_refs = refs[0:6]
    weights, out_ref, held, sums, sems = refs[6:]
    tiles, fields, _ = piece_refs[0].shape
    chunks = 4
    tiles_chunk = tiles // chunks
    per_row, total_rows, _ = sums.shape
    rows = total_rows // fields
    copies = [
        pltpu.make_async_copy(source, held.at[pl.ds(index * tiles, tiles)], sems.at[index])
        for index, source in enumerate(piece_refs)
    ]
    for copy in copies:
        copy.start()
    for copy in copies:
        copy.wait()

    @pl.loop(0, chunks)
    def _(chunk):
        for pair in range(tiles_chunk // 2):
            first = chunk * tiles_chunk + 2 * pair
            lefts = []
            for item in range(2):
                base = (first + item) * OV
                lefts.append(
                    jnp.concatenate([held[position_ref[base + slot]] for slot in range(OV)], axis=1)
                )
            left = jnp.concatenate(lefts, axis=0)
            right = jnp.concatenate([weights[first], weights[first + 1]], axis=1)
            result = jnp.dot(left, right, preferred_element_type=F32)
            for item in range(2):
                tile = 2 * pair + item
                row = chunk * (tiles_chunk // per_row) + tile // per_row
                sums[tile % per_row, pl.ds(row, fields, stride=rows), :] = result[
                    item * fields : (item + 1) * fields, item * TC : (item + 1) * TC
                ]

    for index in range(per_row):
        out_ref[:, index * TC : (index + 1) * TC] = sums[index].astype(BF16)


def in_hbm(value):
    return pltpu.with_memory_space_constraint(value, pltpu.HBM)


def on_device(
    column_state,
    forcing,
    couple_gain,
    diffusion,
    mixing,
    export_map,
    land_mask,
    sources,
    regrid_weights,
):
    shard = lax.axis_index("blk")
    count = lax.axis_size("blk")
    _, levels, rows, columns = column_state.shape
    fields = forcing.shape[1]
    tiles = rows * columns // TC
    per_row = columns // TC
    inner_rows = rows - 2 * EDGE
    inner_tiles = inner_rows * per_row
    state = in_hbm(column_state[0])
    force = in_hbm(forcing.reshape(fields * rows, columns))
    gain = in_hbm(couple_gain[0].T)
    land_mask = in_hbm(land_mask)
    rate = diffusion
    mixer = mixing[0]
    export = export_map[0]
    whole = pl.BlockSpec(memory_space=VMEM)
    anywhere = pl.BlockSpec(memory_space=pl.ANY)

    payload = levels * EDGE + 16
    down, up = pl.pallas_call(
        edge_kernel,
        grid=(1,),
        in_specs=[
            pl.BlockSpec((levels, 8, TC), lambda i, j=index, k=k: (0, k, j))
            for k in (0, rows // 8 - 1)
            for index in range(per_row)
        ]
        + [
            pl.BlockSpec((fields * rows, columns), lambda i: (0, 0)),
            pl.BlockSpec((fields, levels), lambda i: (0, 0)),
            pl.BlockSpec((rows, columns), lambda i: (0, 0)),
        ],
        out_specs=[pl.BlockSpec((payload, columns), lambda i: (0, 0))] * 2,
        out_shape=[jax.ShapeDtypeStruct((payload, columns), BF16)] * 2,
        scratch_shapes=[VMEM((per_row, fields * rows, TC), F32)],
        compiler_params=pltpu.CompilerParams(vmem_limit_bytes=16 * MIB),
        cost_estimate=pl.CostEstimate(flops=10**7, bytes_accessed=3 * MIB, transcendentals=0),
        name="edges",
    )(*[state] * (2 * per_row), force, gain, land_mask)
    upward = [(i, i + 1) for i in range(count - 1)]
    downward = [(i + 1, i) for i in range(count - 1)]
    low = lax.ppermute(up, "blk", upward)
    high = lax.ppermute(down, "blk", downward)

    inner_final, edges, inner_surface = pl.pallas_call(
        inner_kernel,
        in_specs=[pl.BlockSpec(memory_space=pl.ANY)] + [whole] * 6,
        out_specs=[whole] * 3,
        out_shape=[
            VMEM((inner_rows, levels, columns), F32),
            VMEM((2, NSTEP, 2, levels, columns), F32),
            VMEM((inner_tiles, fields, TC), BF16),
        ],
        scratch_shapes=[
            VMEM((rows, levels, columns), F32),
            VMEM((rows, levels, columns), F32),
            VMEM((rows // 8, per_row, levels, 8, TC), F32),
            VMEM((per_row, fields * rows, TC), F32),
            VMEM((rows, columns), F32),
            pltpu.SemaphoreType.DMA((rows // 8, per_row)),
        ],
        compiler_params=pltpu.CompilerParams(vmem_limit_bytes=18 * MIB),
        cost_estimate=pl.CostEstimate(flops=10**10, bytes_accessed=20 * MIB, transcendentals=0),
        name="inner",
    )(state, force, gain, rate, mixer, export, land_mask)

    outer_final, surface = pl.pallas_call(
        outer_kernel,
        in_specs=[whole] * 8,
        out_specs=[whole] * 2,
        out_shape=[
            VMEM((2, EDGE, levels, columns), F32),
            VMEM((tiles, fields, TC), BF16),
        ],
        scratch_shapes=[
            VMEM((2, EDGE + 2, levels, columns), F32),
            VMEM((2, EDGE + 2, levels, columns), F32),
            VMEM((2, 2 * EDGE, columns), F32),
        ],
        compiler_params=pltpu.CompilerParams(vmem_limit_bytes=16 * MIB),
        cost_estimate=pl.CostEstimate(flops=3 * 10**9, bytes_accessed=4 * MIB, transcendentals=0),
        name="outer",
    )(low, high, edges, rate, mixer, export, land_mask, inner_surface)

    section_count = lax.axis_size("sec")
    across = [(i, section_count - 1 - i) for i in range(section_count)]
    later = [(i, (i + 2) % count) for i in range(count)]
    earlier = [(i, (i - 2) % count) for i in range(count)]
    mates = [(i, i ^ 1) for i in range(count)]

    core = shard % 2
    wanted = sources.reshape(-1)
    away = wanted // tiles - (shard - core) + 2
    away = away % count
    same_core = away % 2 == core
    positions = (jnp.where(same_core, 0, 3) + away // 2) * tiles + wanted % tiles

    weights = in_hbm(regrid_weights.reshape(tiles, OV * TC, TC))

    raw = regrid_weights.reshape(tiles, OV * TC, TC)
    raw, surface = lax.optimization_barrier((raw, surface))
    here = lax.ppermute(surface, "sec", across)
    weights = pl.pallas_call(
        load_kernel,
        in_specs=[anywhere],
        out_specs=whole,
        out_shape=VMEM((tiles, OV * TC, TC), BF16),
        scratch_shapes=[pltpu.SemaphoreType.DMA((16,))],
        compiler_params=pltpu.CompilerParams(vmem_limit_bytes=16 * MIB),
        cost_estimate=pl.CostEstimate(flops=0, bytes_accessed=12 * MIB, transcendentals=0),
        name="load",
    )(in_hbm(raw))
    here, positions, inner_final, outer_final, weights = lax.optimization_barrier(
        (here, positions, inner_final, outer_final, weights)
    )
    before = lax.ppermute(here, "blk", later)
    after = lax.ppermute(here, "blk", earlier)
    new_state = pl.pallas_call(
        write_kernel,
        grid=(per_row,),
        in_specs=[
            pl.BlockSpec((inner_rows, levels, TC), lambda j: (0, 0, j)),
            pl.BlockSpec((2, EDGE, levels, TC), lambda j: (0, 0, 0, j)),
        ],
        out_specs=pl.BlockSpec((levels * rows, TC), lambda j: (0, j)),
        out_shape=jax.ShapeDtypeStruct((levels * rows, columns), F32),
        compiler_params=pltpu.CompilerParams(vmem_limit_bytes=8 * MIB),
        cost_estimate=pl.CostEstimate(flops=0, bytes_accessed=8 * MIB, transcendentals=0),
        name="write",
    )(inner_final, outer_final)
    late, new_state = lax.optimization_barrier((here, new_state))
    other = lax.ppermute(late, "blk", mates)
    pieces = [before, here, after]
    pieces += [lax.ppermute(before, "blk", mates), other, lax.ppermute(after, "blk", mates)]

    coupled = pl.pallas_call(
        regrid_kernel,
        grid_spec=pltpu.PrefetchScalarGridSpec(
            num_scalar_prefetch=1,
            grid=(1,),
            in_specs=[anywhere] * 6 + [whole],
            out_specs=pl.BlockSpec((fields * rows, columns), lambda i, p: (0, 0)),
            scratch_shapes=[
                VMEM((6 * tiles, fields, TC), BF16),
                VMEM((per_row, fields * rows, TC), F32),
                pltpu.SemaphoreType.DMA((6,)),
            ],
        ),
        out_shape=jax.ShapeDtypeStruct((fields * rows, columns), BF16),
        compiler_params=pltpu.CompilerParams(vmem_limit_bytes=8 * MIB),
        cost_estimate=pl.CostEstimate(flops=10**9, bytes_accessed=16 * MIB, transcendentals=0),
        name="regrid",
    )(positions, *pieces, weights)

    return (
        new_state.reshape(1, levels, rows, columns),
        coupled.reshape(1, fields, rows, columns),
    )


def solution(mesh):
    in_specs = (
        P("sec", None, "blk", None),
        P("sec", None, "blk", None),
        P("sec", None, None),
        P("sec", None),
        P("sec", None, None),
        P("sec", None, None),
        P("blk", None),
        P("sec", "blk", None),
        P("sec", "blk", None, None, None),
    )
    out_specs = (P("sec", None, "blk", None), P("sec", None, "blk", None))
    return jax.shard_map(
        on_device, mesh=mesh, in_specs=in_specs, out_specs=out_specs, check_vma=False
    )
```

```python
import jax
import jax.numpy as jnp
from jax import lax
from jax.experimental import pallas as pl
from jax.experimental.pallas import tpu as pltpu
from jax.sharding import PartitionSpec as P

TC = 128
OV = 3
REACH = 2
NSTEP = 4
EDGE = NSTEP
F32 = jnp.float32
BF16 = jnp.bfloat16
VMEM = pltpu.VMEM
MIB = 2**20


def split(value):
    high = value.astype(BF16)
    return high, (value - high.astype(F32)).astype(BF16)


def column(row):
    n = row.shape[1]
    eye = lax.broadcasted_iota(jnp.int32, (n, n), 0) == lax.broadcasted_iota(jnp.int32, (n, n), 1)
    return jnp.sum(jnp.where(eye, jnp.broadcast_to(row, (n, n)), 0.0), axis=1, keepdims=True)


def stacked(matrix):
    high, low = split(matrix)
    return jnp.concatenate([high, high, low], axis=1)


def mixers(mixing, export_map):
    n = mixing.shape[0]
    eye = lax.broadcasted_iota(jnp.int32, (n, n), 0) == lax.broadcasted_iota(jnp.int32, (n, n), 1)
    step = 0.5 * (jnp.where(eye, 1.0, 0.0) + mixing)
    out = jnp.dot(export_map, step, precision=lax.Precision.HIGHEST, preferred_element_type=F32)
    return stacked(jnp.concatenate([step, out], axis=0))


def rows_of(blocks, first, size, stride):
    return jnp.concatenate([block[pl.ds(first, size, stride=stride), :] for block in blocks], axis=1)


def driven(gain, pushed):
    return lax.dot_general(gain, pushed, (((0,), (0,)), ((), ())), preferred_element_type=F32)


def wetness_of(mask):
    return jnp.where((mask > 0) | (lax.axis_index("sec") != 1), 1.0, 0.0)


def blocks_of(ref):
    return [ref.at[index] for index in range(ref.shape[0])]


def diffused(here, above, below, wet, rate):
    columns = here.shape[1]
    rounded = here.astype(BF16)
    sides = pltpu.roll(rounded, 1, 1) + pltpu.roll(rounded, columns - 1, 1)
    near = (above + below) + sides.astype(F32)
    return here + wet * (rate * (near - 4.0 * here))


def mixed(factor, value):
    high, low = split(value)
    return jnp.dot(factor, jnp.concatenate([high, low, high], axis=0), preferred_element_type=F32)


def load_force(forcing_ref, force):
    value = forcing_ref[...].astype(F32)
    for index in range(force.shape[0]):
        force[index] = value[:, index * TC : (index + 1) * TC]


def edge_kernel(*refs):
    forcing_ref, gain_ref, mask_ref, down_ref, up_ref, force = refs[-6:]
    blocks = (len(refs) - 6) // 2
    top_refs = refs[:blocks]
    bottom_refs = refs[blocks : 2 * blocks]
    fields, levels = gain_ref.shape
    columns = forcing_ref.shape[1]
    rows = forcing_ref.shape[0] // fields
    load_force(forcing_ref, force)
    gain = gain_ref[...]
    for state_refs, out_ref, first, inside in (
        (top_refs, down_ref, 0, 0),
        (bottom_refs, up_ref, rows - EDGE, 8 - EDGE),
    ):
        state = [ref.reshape(levels * 8, TC) for ref in state_refs]
        for row in range(EDGE):
            pushed = rows_of(blocks_of(force), first + row, fields, rows).astype(BF16)
            value = rows_of(state, inside + row, levels, 8) + driven(gain, pushed)
            out_ref[levels * row : levels * (row + 1), :] = value.astype(BF16)
        out_ref[levels * EDGE :, :] = jnp.concatenate(
            [wetness_of(mask_ref[first : first + EDGE, :]), jnp.zeros((16 - EDGE, columns), F32)], axis=0
        ).astype(BF16)


def inner_kernel(
    state_ref,
    forcing_ref,
    gain_ref,
    rate_ref,
    mixing_ref,
    export_ref,
    mask_ref,
    final_ref,
    edge_ref,
    surface_ref,
    even,
    odd,
    arrived,
    force,
    wet_ref,
    sems,
):
    fields, levels = gain_ref.shape
    rows, columns = mask_ref.shape
    blocks = columns // TC

    def arrival(group, block):
        return pltpu.make_async_copy(
            state_ref.at[:, pl.ds(group * 8, 8), pl.ds(block * TC, TC)],
            arrived.at[group, block],
            sems.at[group, block],
        )

    for group in range(rows // 8):
        for block in range(blocks):
            arrival(group, block).start()
    load_force(forcing_ref, force)
    wet_ref[...] = wetness_of(mask_ref[...])
    gain = gain_ref[...]
    rate = column(rate_ref[...])
    factor = mixers(mixing_ref[...], export_ref[...])
    step_factor = factor[:levels]

    for group in range(rows // 8):
        for block in range(blocks):
            arrival(group, block).wait()
        state = [arrived.at[group, block].reshape(levels * 8, TC) for block in range(blocks)]
        for part in range(8):
            row = group * 8 + part
            pushed = rows_of(blocks_of(force), row, fields, rows).astype(BF16)
            even[row] = rows_of(state, part, levels, 8) + driven(gain, pushed)

    for step in range(1, NSTEP + 1):
        source, target = (even, odd) if step % 2 else (odd, even)
        last = step == NSTEP


        for row in range(step, rows - step):
            value = diffused(
                source[row],
                source[row - 1],
                source[row + 1],
                wet_ref[row : row + 1, :],
                rate,
            )
            result = mixed(factor if last else step_factor, value)
            if last:
                final_ref[row - EDGE] = result[:levels]
                surface = jnp.tanh(result[levels:]).astype(BF16)
                per_row = columns // TC
                for tile in range(per_row):
                    surface_ref[(row - EDGE) * per_row + tile] = surface[
                        :, tile * TC : (tile + 1) * TC
                    ]
            else:
                target[row] = result

    for step in range(NSTEP):
        source = odd if step % 2 else even
        edge_ref[0, step, 0] = source[step]
        edge_ref[0, step, 1] = source[step + 1]
        edge_ref[1, step, 0] = source[rows - 2 - step]
        edge_ref[1, step, 1] = source[rows - 1 - step]


def outer_kernel(
    low_ref,
    high_ref,
    edge_ref,
    rate_ref,
    mixing_ref,
    export_ref,
    mask_ref,
    inner_ref,
    final_ref,
    surface_ref,
    even,
    odd,
    wet,
):
    levels = mixing_ref.shape[0]
    rows, columns = mask_ref.shape
    inner_tiles = inner_ref.shape[0]
    per_row = columns // TC
    rate = column(rate_ref[...])
    factor = mixers(mixing_ref[...], export_ref[...])
    step_factor = factor[:levels]
    wet[0, 0:EDGE, :] = low_ref[levels * EDGE :, :].astype(F32)[0:EDGE]
    wet[0, EDGE : 2 * EDGE, :] = wetness_of(mask_ref[0:EDGE, :])
    wet[1, 0:EDGE, :] = wetness_of(mask_ref[rows - EDGE : rows, :])
    surface_ref[pl.ds(EDGE * per_row, inner_tiles)] = inner_ref[...]
    wet[1, EDGE : 2 * EDGE, :] = high_ref[levels * EDGE :, :].astype(F32)[0:EDGE]
    for row in range(EDGE):
        even[0, row] = low_ref[levels * row : levels * (row + 1), :].astype(F32)
        even[1, row + 2] = high_ref[levels * row : levels * (row + 1), :].astype(F32)
    for step in range(1, NSTEP + 1):
        source, target = (even, odd) if step % 2 else (odd, even)
        last = step == NSTEP
        for item in range(2):
            source[0, EDGE + item] = edge_ref[0, step - 1, item]
            source[1, item] = edge_ref[1, step - 1, item]
        for side in range(2):
            first_wet = step if side == 0 else NSTEP - step
            shift = 0 if side == 0 else 2
            for row in range(EDGE):
                value = diffused(
                    source[side, row + 1],
                    source[side, row],
                    source[side, row + 2],
                    wet[side, first_wet + row : first_wet + row + 1, :],
                    rate,
                )
                result = mixed(factor if last else step_factor, value)
                if last:
                    final_ref[side, row] = result[:levels]
                    surface = jnp.tanh(result[levels:]).astype(BF16)
                    for tile in range(per_row):
                        surface_ref[(side * (rows - EDGE) + row) * per_row + tile] = surface[
                            :, tile * TC : (tile + 1) * TC
                        ]
                else:
                    target[side, row + shift] = result


def write_kernel(inner_ref, outer_ref, state_ref):
    levels = inner_ref.shape[1]
    rows = inner_ref.shape[0] + 2 * EDGE

    for row in range(EDGE):
        state_ref[pl.ds(row, levels, stride=rows), :] = outer_ref[0, row]
        state_ref[pl.ds(rows - EDGE + row, levels, stride=rows), :] = outer_ref[1, row]

    @pl.loop(0, rows - 2 * EDGE)
    def _(row):
        state_ref[pl.ds(row + EDGE, levels, stride=rows), :] = inner_ref[row]


def load_kernel(source_ref, target_ref, sems):
    chunks = sems.shape[0]
    size = source_ref.shape[0] // chunks
    copies = [
        pltpu.make_async_copy(
            source_ref.at[pl.ds(chunk * size, size)],
            target_ref.at[pl.ds(chunk * size, size)],
            sems.at[chunk],
        )
        for chunk in range(chunks)
    ]
    for copy in copies:
        copy.start()
    for copy in copies:
        copy.wait()


def regrid_kernel(position_ref, *refs):
    piece_refs = refs[0:6]
    weights, out_ref, held, sums, sems = refs[6:]
    tiles, fields, _ = piece_refs[0].shape
    chunks = 1
    tiles_chunk = tiles // chunks
    per_row, total_rows, _ = sums.shape
    rows = total_rows // fields
    copies = [
        pltpu.make_async_copy(source, held.at[pl.ds(index * tiles, tiles)], sems.at[index])
        for index, source in enumerate(piece_refs)
    ]
    for copy in copies:
        copy.start()
    for copy in copies:
        copy.wait()

    for chunk in range(chunks):
        for pair in range(tiles_chunk // 2):
            first = chunk * tiles_chunk + 2 * pair
            lefts = []
            for item in range(2):
                base = (first + item) * OV
                lefts.append(
                    jnp.concatenate([held[position_ref[base + slot]] for slot in range(OV)], axis=1)
                )
            left = jnp.concatenate(lefts, axis=0)
            right = jnp.concatenate([weights[first], weights[first + 1]], axis=1)
            result = jnp.dot(left, right, preferred_element_type=F32)
            for item in range(2):
                tile = 2 * pair + item
                row = chunk * (tiles_chunk // per_row) + tile // per_row
                sums[tile % per_row, pl.ds(row, fields, stride=rows), :] = result[
                    item * fields : (item + 1) * fields, item * TC : (item + 1) * TC
                ]

    for index in range(per_row):
        out_ref[:, index * TC : (index + 1) * TC] = sums[index].astype(BF16)


def in_hbm(value):
    return pltpu.with_memory_space_constraint(value, pltpu.HBM)


def on_device(
    column_state,
    forcing,
    couple_gain,
    diffusion,
    mixing,
    export_map,
    land_mask,
    sources,
    regrid_weights,
):
    shard = lax.axis_index("blk")
    count = lax.axis_size("blk")
    _, levels, rows, columns = column_state.shape
    fields = forcing.shape[1]
    tiles = rows * columns // TC
    per_row = columns // TC
    inner_rows = rows - 2 * EDGE
    inner_tiles = inner_rows * per_row
    state = in_hbm(column_state[0])
    force = in_hbm(forcing.reshape(fields * rows, columns))
    gain = in_hbm(couple_gain[0].T)
    land_mask = in_hbm(land_mask)
    rate = diffusion
    mixer = mixing[0]
    export = export_map[0]
    whole = pl.BlockSpec(memory_space=VMEM)
    anywhere = pl.BlockSpec(memory_space=pl.ANY)

    payload = levels * EDGE + 16
    down, up = pl.pallas_call(
        edge_kernel,
        grid=(1,),
        in_specs=[
            pl.BlockSpec((levels, 8, TC), lambda i, j=index, k=k: (0, k, j))
            for k in (0, rows // 8 - 1)
            for index in range(per_row)
        ]
        + [
            pl.BlockSpec((fields * rows, columns), lambda i: (0, 0)),
            pl.BlockSpec((fields, levels), lambda i: (0, 0)),
            pl.BlockSpec((rows, columns), lambda i: (0, 0)),
        ],
        out_specs=[pl.BlockSpec((payload, columns), lambda i: (0, 0))] * 2,
        out_shape=[jax.ShapeDtypeStruct((payload, columns), BF16)] * 2,
        scratch_shapes=[VMEM((per_row, fields * rows, TC), F32)],
        compiler_params=pltpu.CompilerParams(vmem_limit_bytes=16 * MIB),
        cost_estimate=pl.CostEstimate(flops=10**7, bytes_accessed=3 * MIB, transcendentals=0),
        name="edges",
    )(*[state] * (2 * per_row), force, gain, land_mask)
    upward = [(i, i + 1) for i in range(count - 1)]
    downward = [(i + 1, i) for i in range(count - 1)]
    low = lax.ppermute(up, "blk", upward)
    high = lax.ppermute(down, "blk", downward)

    inner_final, edges, inner_surface = pl.pallas_call(
        inner_kernel,
        in_specs=[pl.BlockSpec(memory_space=pl.ANY)] + [whole] * 6,
        out_specs=[whole] * 3,
        out_shape=[
            VMEM((inner_rows, levels, columns), F32),
            VMEM((2, NSTEP, 2, levels, columns), F32),
            VMEM((inner_tiles, fields, TC), BF16),
        ],
        scratch_shapes=[
            VMEM((rows, levels, columns), F32),
            VMEM((rows, levels, columns), F32),
            VMEM((rows // 8, per_row, levels, 8, TC), F32),
            VMEM((per_row, fields * rows, TC), F32),
            VMEM((rows, columns), F32),
            pltpu.SemaphoreType.DMA((rows // 8, per_row)),
        ],
        compiler_params=pltpu.CompilerParams(vmem_limit_bytes=18 * MIB),
        cost_estimate=pl.CostEstimate(flops=10**10, bytes_accessed=20 * MIB, transcendentals=0),
        name="inner",
    )(state, force, gain, rate, mixer, export, land_mask)

    outer_final, surface = pl.pallas_call(
        outer_kernel,
        in_specs=[whole] * 8,
        out_specs=[whole] * 2,
        out_shape=[
            VMEM((2, EDGE, levels, columns), F32),
            VMEM((tiles, fields, TC), BF16),
        ],
        scratch_shapes=[
            VMEM((2, EDGE + 2, levels, columns), F32),
            VMEM((2, EDGE + 2, levels, columns), F32),
            VMEM((2, 2 * EDGE, columns), F32),
        ],
        compiler_params=pltpu.CompilerParams(vmem_limit_bytes=16 * MIB),
        cost_estimate=pl.CostEstimate(flops=3 * 10**9, bytes_accessed=4 * MIB, transcendentals=0),
        name="outer",
    )(low, high, edges, rate, mixer, export, land_mask, inner_surface)

    section_count = lax.axis_size("sec")
    across = [(i, section_count - 1 - i) for i in range(section_count)]
    later = [(i, (i + 2) % count) for i in range(count)]
    earlier = [(i, (i - 2) % count) for i in range(count)]
    mates = [(i, i ^ 1) for i in range(count)]

    core = shard % 2
    wanted = sources.reshape(-1)
    away = wanted // tiles - (shard - core) + 2
    away = away % count
    same_core = away % 2 == core
    positions = (jnp.where(same_core, 0, 3) + away // 2) * tiles + wanted % tiles

    weights = in_hbm(regrid_weights.reshape(tiles, OV * TC, TC))

    raw = regrid_weights.reshape(tiles, OV * TC, TC)
    raw, surface = lax.optimization_barrier((raw, surface))
    here = lax.ppermute(surface, "sec", across)
    weights = pl.pallas_call(
        load_kernel,
        in_specs=[anywhere],
        out_specs=whole,
        out_shape=VMEM((tiles, OV * TC, TC), BF16),
        scratch_shapes=[pltpu.SemaphoreType.DMA((16,))],
        compiler_params=pltpu.CompilerParams(vmem_limit_bytes=16 * MIB),
        cost_estimate=pl.CostEstimate(flops=0, bytes_accessed=12 * MIB, transcendentals=0),
        name="load",
    )(in_hbm(raw))
    here, positions, inner_final, outer_final, weights = lax.optimization_barrier(
        (here, positions, inner_final, outer_final, weights)
    )
    before = lax.ppermute(here, "blk", later)
    after = lax.ppermute(here, "blk", earlier)
    new_state = pl.pallas_call(
        write_kernel,
        grid=(per_row,),
        in_specs=[
            pl.BlockSpec((inner_rows, levels, TC), lambda j: (0, 0, j)),
            pl.BlockSpec((2, EDGE, levels, TC), lambda j: (0, 0, 0, j)),
        ],
        out_specs=pl.BlockSpec((levels * rows, TC), lambda j: (0, j)),
        out_shape=jax.ShapeDtypeStruct((levels * rows, columns), F32),
        compiler_params=pltpu.CompilerParams(vmem_limit_bytes=8 * MIB),
        cost_estimate=pl.CostEstimate(flops=0, bytes_accessed=8 * MIB, transcendentals=0),
        name="write",
    )(inner_final, outer_final)
    late, new_state = lax.optimization_barrier((here, new_state))
    other = lax.ppermute(late, "blk", mates)
    pieces = [before, here, after]
    pieces += [lax.ppermute(before, "blk", mates), other, lax.ppermute(after, "blk", mates)]

    coupled = pl.pallas_call(
        regrid_kernel,
        grid_spec=pltpu.PrefetchScalarGridSpec(
            num_scalar_prefetch=1,
            grid=(1,),
            in_specs=[anywhere] * 6 + [whole],
            out_specs=pl.BlockSpec((fields * rows, columns), lambda i, p: (0, 0)),
            scratch_shapes=[
                VMEM((6 * tiles, fields, TC), BF16),
                VMEM((per_row, fields * rows, TC), F32),
                pltpu.SemaphoreType.DMA((6,)),
            ],
        ),
        out_shape=jax.ShapeDtypeStruct((fields * rows, columns), BF16),
        compiler_params=pltpu.CompilerParams(vmem_limit_bytes=8 * MIB),
        cost_estimate=pl.CostEstimate(flops=10**9, bytes_accessed=16 * MIB, transcendentals=0),
        name="regrid",
    )(positions, *pieces, weights)

    return (
        new_state.reshape(1, levels, rows, columns),
        coupled.reshape(1, fields, rows, columns),
    )


def solution(mesh):
    in_specs = (
        P("sec", None, "blk", None),
        P("sec", None, "blk", None),
        P("sec", None, None),
        P("sec", None),
        P("sec", None, None),
        P("sec", None, None),
        P("blk", None),
        P("sec", "blk", None),
        P("sec", "blk", None, None, None),
    )
    out_specs = (P("sec", None, "blk", None), P("sec", None, "blk", None))
    return jax.shard_map(
        on_device, mesh=mesh, in_specs=in_specs, out_specs=out_specs, check_vma=False
    )
```

```python
import jax
import jax.numpy as jnp
from jax import lax
from jax.experimental import pallas as pl
from jax.experimental.pallas import tpu as pltpu
from jax.sharding import PartitionSpec as P

TC = 128
OV = 3
REACH = 2
NSTEP = 4
EDGE = NSTEP
F32 = jnp.float32
BF16 = jnp.bfloat16
VMEM = pltpu.VMEM
MIB = 2**20


def split(value):
    high = value.astype(BF16)
    return high, (value - high.astype(F32)).astype(BF16)


def column(row):
    n = row.shape[1]
    eye = lax.broadcasted_iota(jnp.int32, (n, n), 0) == lax.broadcasted_iota(jnp.int32, (n, n), 1)
    return jnp.sum(jnp.where(eye, jnp.broadcast_to(row, (n, n)), 0.0), axis=1, keepdims=True)


def stacked(matrix):
    high, low = split(matrix)
    return jnp.concatenate([high, high, low], axis=1)


def mixers(mixing, export_map):
    n = mixing.shape[0]
    eye = lax.broadcasted_iota(jnp.int32, (n, n), 0) == lax.broadcasted_iota(jnp.int32, (n, n), 1)
    step = 0.5 * (jnp.where(eye, 1.0, 0.0) + mixing)
    out = jnp.dot(export_map, step, precision=lax.Precision.HIGHEST, preferred_element_type=F32)
    return stacked(jnp.concatenate([step, out], axis=0))


def rows_of(blocks, first, size, stride):
    return jnp.concatenate([block[pl.ds(first, size, stride=stride), :] for block in blocks], axis=1)


def driven(gain, pushed):
    return lax.dot_general(gain, pushed, (((0,), (0,)), ((), ())), preferred_element_type=F32)


def wetness_of(mask):
    return jnp.where((mask > 0) | (lax.axis_index("sec") != 1), 1.0, 0.0)


def blocks_of(ref):
    return [ref.at[index] for index in range(ref.shape[0])]


def diffused(here, above, below, wet, rate):
    columns = here.shape[1]
    rounded = here.astype(BF16)
    sides = pltpu.roll(rounded, 1, 1) + pltpu.roll(rounded, columns - 1, 1)
    near = (above + below) + sides.astype(F32)
    return here + wet * (rate * (near - 4.0 * here))


def mixed(factor, value):
    high, low = split(value)
    return jnp.dot(factor, jnp.concatenate([high, low, high], axis=0), preferred_element_type=F32)


def load_force(forcing_ref, force):
    value = forcing_ref[...].astype(F32)
    for index in range(force.shape[0]):
        force[index] = value[:, index * TC : (index + 1) * TC]


def edge_kernel(*refs):
    forcing_ref, gain_ref, mask_ref, down_ref, up_ref, force = refs[-6:]
    blocks = (len(refs) - 6) // 2
    top_refs = refs[:blocks]
    bottom_refs = refs[blocks : 2 * blocks]
    fields, levels = gain_ref.shape
    columns = forcing_ref.shape[1]
    rows = forcing_ref.shape[0] // fields
    load_force(forcing_ref, force)
    gain = gain_ref[...]
    for state_refs, out_ref, first, inside in (
        (top_refs, down_ref, 0, 0),
        (bottom_refs, up_ref, rows - EDGE, 8 - EDGE),
    ):
        state = [ref.reshape(levels * 8, TC) for ref in state_refs]
        for row in range(EDGE):
            pushed = rows_of(blocks_of(force), first + row, fields, rows).astype(BF16)
            value = rows_of(state, inside + row, levels, 8) + driven(gain, pushed)
            out_ref[levels * row : levels * (row + 1), :] = value.astype(BF16)
        out_ref[levels * EDGE :, :] = jnp.concatenate(
            [wetness_of(mask_ref[first : first + EDGE, :]), jnp.zeros((16 - EDGE, columns), F32)], axis=0
        ).astype(BF16)


def inner_kernel(
    state_ref,
    forcing_ref,
    gain_ref,
    rate_ref,
    mixing_ref,
    export_ref,
    mask_ref,
    final_ref,
    edge_ref,
    surface_ref,
    even,
    odd,
    arrived,
    force,
    wet_ref,
    sems,
):
    fields, levels = gain_ref.shape
    rows, columns = mask_ref.shape
    blocks = columns // TC

    def arrival(group, block):
        return pltpu.make_async_copy(
            state_ref.at[:, pl.ds(group * 8, 8), pl.ds(block * TC, TC)],
            arrived.at[group, block],
            sems.at[group, block],
        )

    for group in range(rows // 8):
        for block in range(blocks):
            arrival(group, block).start()
    load_force(forcing_ref, force)
    wet_ref[...] = wetness_of(mask_ref[...])
    gain = gain_ref[...]
    rate = column(rate_ref[...])
    factor = mixers(mixing_ref[...], export_ref[...])
    step_factor = factor[:levels]

    for group in range(rows // 8):
        for block in range(blocks):
            arrival(group, block).wait()
        state = [arrived.at[group, block].reshape(levels * 8, TC) for block in range(blocks)]
        for part in range(8):
            row = group * 8 + part
            pushed = rows_of(blocks_of(force), row, fields, rows).astype(BF16)
            even[row] = rows_of(state, part, levels, 8) + driven(gain, pushed)
        for row in range(max(1, group * 8 - 1), group * 8 + 7):
            odd[row] = mixed(
                step_factor,
                diffused(even[row], even[row - 1], even[row + 1], wet_ref[row : row + 1, :], rate),
            )

    for step in range(2, NSTEP + 1):
        source, target = (even, odd) if step % 2 else (odd, even)
        last = step == NSTEP


        for row in range(step, rows - step):
            value = diffused(
                source[row],
                source[row - 1],
                source[row + 1],
                wet_ref[row : row + 1, :],
                rate,
            )
            result = mixed(factor if last else step_factor, value)
            if last:
                final_ref[row - EDGE] = result[:levels]
                surface = jnp.tanh(result[levels:]).astype(BF16)
                per_row = columns // TC
                for tile in range(per_row):
                    surface_ref[(row - EDGE) * per_row + tile] = surface[
                        :, tile * TC : (tile + 1) * TC
                    ]
            else:
                target[row] = result

    for step in range(NSTEP):
        source = odd if step % 2 else even
        edge_ref[0, step, 0] = source[step]
        edge_ref[0, step, 1] = source[step + 1]
        edge_ref[1, step, 0] = source[rows - 2 - step]
        edge_ref[1, step, 1] = source[rows - 1 - step]


def outer_kernel(
    low_ref,
    high_ref,
    edge_ref,
    rate_ref,
    mixing_ref,
    export_ref,
    mask_ref,
    inner_ref,
    final_ref,
    surface_ref,
    even,
    odd,
    wet,
):
    levels = mixing_ref.shape[0]
    rows, columns = mask_ref.shape
    inner_tiles = inner_ref.shape[0]
    per_row = columns // TC
    rate = column(rate_ref[...])
    factor = mixers(mixing_ref[...], export_ref[...])
    step_factor = factor[:levels]
    wet[0, 0:EDGE, :] = low_ref[levels * EDGE :, :].astype(F32)[0:EDGE]
    wet[0, EDGE : 2 * EDGE, :] = wetness_of(mask_ref[0:EDGE, :])
    wet[1, 0:EDGE, :] = wetness_of(mask_ref[rows - EDGE : rows, :])
    surface_ref[pl.ds(EDGE * per_row, inner_tiles)] = inner_ref[...]
    wet[1, EDGE : 2 * EDGE, :] = high_ref[levels * EDGE :, :].astype(F32)[0:EDGE]
    for row in range(EDGE):
        even[0, row] = low_ref[levels * row : levels * (row + 1), :].astype(F32)
        even[1, row + 2] = high_ref[levels * row : levels * (row + 1), :].astype(F32)
    for step in range(1, NSTEP + 1):
        source, target = (even, odd) if step % 2 else (odd, even)
        last = step == NSTEP
        for item in range(2):
            source[0, EDGE + item] = edge_ref[0, step - 1, item]
            source[1, item] = edge_ref[1, step - 1, item]
        for side in range(2):
            first_wet = step if side == 0 else NSTEP - step
            shift = 0 if side == 0 else 2
            for row in range(EDGE):
                value = diffused(
                    source[side, row + 1],
                    source[side, row],
                    source[side, row + 2],
                    wet[side, first_wet + row : first_wet + row + 1, :],
                    rate,
                )
                result = mixed(factor if last else step_factor, value)
                if last:
                    final_ref[side, row] = result[:levels]
                    surface = jnp.tanh(result[levels:]).astype(BF16)
                    for tile in range(per_row):
                        surface_ref[(side * (rows - EDGE) + row) * per_row + tile] = surface[
                            :, tile * TC : (tile + 1) * TC
                        ]
                else:
                    target[side, row + shift] = result


def write_kernel(inner_ref, outer_ref, state_ref):
    levels = inner_ref.shape[1]
    rows = inner_ref.shape[0] + 2 * EDGE

    for row in range(EDGE):
        state_ref[pl.ds(row, levels, stride=rows), :] = outer_ref[0, row]
        state_ref[pl.ds(rows - EDGE + row, levels, stride=rows), :] = outer_ref[1, row]

    @pl.loop(0, rows - 2 * EDGE)
    def _(row):
        state_ref[pl.ds(row + EDGE, levels, stride=rows), :] = inner_ref[row]


def load_kernel(source_ref, target_ref, sems):
    chunks = sems.shape[0]
    size = source_ref.shape[0] // chunks
    copies = [
        pltpu.make_async_copy(
            source_ref.at[pl.ds(chunk * size, size)],
            target_ref.at[pl.ds(chunk * size, size)],
            sems.at[chunk],
        )
        for chunk in range(chunks)
    ]
    for copy in copies:
        copy.start()
    for copy in copies:
        copy.wait()


def regrid_kernel(position_ref, *refs):
    piece_refs = refs[0:6]
    weights, out_ref, held, sums, sems = refs[6:]
    tiles, fields, _ = piece_refs[0].shape
    chunks = 1
    tiles_chunk = tiles // chunks
    per_row, total_rows, _ = sums.shape
    rows = total_rows // fields
    copies = [
        pltpu.make_async_copy(source, held.at[pl.ds(index * tiles, tiles)], sems.at[index])
        for index, source in enumerate(piece_refs)
    ]
    for copy in copies:
        copy.start()
    for copy in copies:
        copy.wait()

    for chunk in range(chunks):
        for pair in range(tiles_chunk // 2):
            first = chunk * tiles_chunk + 2 * pair
            lefts = []
            for item in range(2):
                base = (first + item) * OV
                lefts.append(
                    jnp.concatenate([held[position_ref[base + slot]] for slot in range(OV)], axis=1)
                )
            left = jnp.concatenate(lefts, axis=0)
            right = jnp.concatenate([weights[first], weights[first + 1]], axis=1)
            result = jnp.dot(left, right, preferred_element_type=F32)
            for item in range(2):
                tile = 2 * pair + item
                row = chunk * (tiles_chunk // per_row) + tile // per_row
                sums[tile % per_row, pl.ds(row, fields, stride=rows), :] = result[
                    item * fields : (item + 1) * fields, item * TC : (item + 1) * TC
                ]

    for index in range(per_row):
        out_ref[:, index * TC : (index + 1) * TC] = sums[index].astype(BF16)


def in_hbm(value):
    return pltpu.with_memory_space_constraint(value, pltpu.HBM)


def on_device(
    column_state,
    forcing,
    couple_gain,
    diffusion,
    mixing,
    export_map,
    land_mask,
    sources,
    regrid_weights,
):
    shard = lax.axis_index("blk")
    count = lax.axis_size("blk")
    _, levels, rows, columns = column_state.shape
    fields = forcing.shape[1]
    tiles = rows * columns // TC
    per_row = columns // TC
    inner_rows = rows - 2 * EDGE
    inner_tiles = inner_rows * per_row
    state = in_hbm(column_state[0])
    force = in_hbm(forcing.reshape(fields * rows, columns))
    gain = in_hbm(couple_gain[0].T)
    land_mask = in_hbm(land_mask)
    rate = diffusion
    mixer = mixing[0]
    export = export_map[0]
    whole = pl.BlockSpec(memory_space=VMEM)
    anywhere = pl.BlockSpec(memory_space=pl.ANY)

    payload = levels * EDGE + 16
    down, up = pl.pallas_call(
        edge_kernel,
        grid=(1,),
        in_specs=[
            pl.BlockSpec((levels, 8, TC), lambda i, j=index, k=k: (0, k, j))
            for k in (0, rows // 8 - 1)
            for index in range(per_row)
        ]
        + [
            pl.BlockSpec((fields * rows, columns), lambda i: (0, 0)),
            pl.BlockSpec((fields, levels), lambda i: (0, 0)),
            pl.BlockSpec((rows, columns), lambda i: (0, 0)),
        ],
        out_specs=[pl.BlockSpec((payload, columns), lambda i: (0, 0))] * 2,
        out_shape=[jax.ShapeDtypeStruct((payload, columns), BF16)] * 2,
        scratch_shapes=[VMEM((per_row, fields * rows, TC), F32)],
        compiler_params=pltpu.CompilerParams(vmem_limit_bytes=16 * MIB),
        cost_estimate=pl.CostEstimate(flops=10**7, bytes_accessed=3 * MIB, transcendentals=0),
        name="edges",
    )(*[state] * (2 * per_row), force, gain, land_mask)
    upward = [(i, i + 1) for i in range(count - 1)]
    downward = [(i + 1, i) for i in range(count - 1)]
    low = lax.ppermute(up, "blk", upward)
    high = lax.ppermute(down, "blk", downward)

    inner_final, edges, inner_surface = pl.pallas_call(
        inner_kernel,
        in_specs=[pl.BlockSpec(memory_space=pl.ANY)] + [whole] * 6,
        out_specs=[whole] * 3,
        out_shape=[
            VMEM((inner_rows, levels, columns), F32),
            VMEM((2, NSTEP, 2, levels, columns), F32),
            VMEM((inner_tiles, fields, TC), BF16),
        ],
        scratch_shapes=[
            VMEM((rows, levels, columns), F32),
            VMEM((rows, levels, columns), F32),
            VMEM((rows // 8, per_row, levels, 8, TC), F32),
            VMEM((per_row, fields * rows, TC), F32),
            VMEM((rows, columns), F32),
            pltpu.SemaphoreType.DMA((rows // 8, per_row)),
        ],
        compiler_params=pltpu.CompilerParams(vmem_limit_bytes=18 * MIB),
        cost_estimate=pl.CostEstimate(flops=10**10, bytes_accessed=20 * MIB, transcendentals=0),
        name="inner",
    )(state, force, gain, rate, mixer, export, land_mask)

    outer_final, surface = pl.pallas_call(
        outer_kernel,
        in_specs=[whole] * 8,
        out_specs=[whole] * 2,
        out_shape=[
            VMEM((2, EDGE, levels, columns), F32),
            VMEM((tiles, fields, TC), BF16),
        ],
        scratch_shapes=[
            VMEM((2, EDGE + 2, levels, columns), F32),
            VMEM((2, EDGE + 2, levels, columns), F32),
            VMEM((2, 2 * EDGE, columns), F32),
        ],
        compiler_params=pltpu.CompilerParams(vmem_limit_bytes=16 * MIB),
        cost_estimate=pl.CostEstimate(flops=3 * 10**9, bytes_accessed=4 * MIB, transcendentals=0),
        name="outer",
    )(low, high, edges, rate, mixer, export, land_mask, inner_surface)

    section_count = lax.axis_size("sec")
    across = [(i, section_count - 1 - i) for i in range(section_count)]
    later = [(i, (i + 2) % count) for i in range(count)]
    earlier = [(i, (i - 2) % count) for i in range(count)]
    mates = [(i, i ^ 1) for i in range(count)]

    core = shard % 2
    wanted = sources.reshape(-1)
    away = wanted // tiles - (shard - core) + 2
    away = away % count
    same_core = away % 2 == core
    positions = (jnp.where(same_core, 0, 3) + away // 2) * tiles + wanted % tiles

    weights = in_hbm(regrid_weights.reshape(tiles, OV * TC, TC))

    raw = regrid_weights.reshape(tiles, OV * TC, TC)
    raw, surface = lax.optimization_barrier((raw, surface))
    here = lax.ppermute(surface, "sec", across)
    weights = pl.pallas_call(
        load_kernel,
        in_specs=[anywhere],
        out_specs=whole,
        out_shape=VMEM((tiles, OV * TC, TC), BF16),
        scratch_shapes=[pltpu.SemaphoreType.DMA((16,))],
        compiler_params=pltpu.CompilerParams(vmem_limit_bytes=16 * MIB),
        cost_estimate=pl.CostEstimate(flops=0, bytes_accessed=12 * MIB, transcendentals=0),
        name="load",
    )(in_hbm(raw))
    here, positions, inner_final, outer_final, weights = lax.optimization_barrier(
        (here, positions, inner_final, outer_final, weights)
    )
    before = lax.ppermute(here, "blk", later)
    after = lax.ppermute(here, "blk", earlier)
    new_state = pl.pallas_call(
        write_kernel,
        grid=(per_row,),
        in_specs=[
            pl.BlockSpec((inner_rows, levels, TC), lambda j: (0, 0, j)),
            pl.BlockSpec((2, EDGE, levels, TC), lambda j: (0, 0, 0, j)),
        ],
        out_specs=pl.BlockSpec((levels * rows, TC), lambda j: (0, j)),
        out_shape=jax.ShapeDtypeStruct((levels * rows, columns), F32),
        compiler_params=pltpu.CompilerParams(vmem_limit_bytes=8 * MIB),
        cost_estimate=pl.CostEstimate(flops=0, bytes_accessed=8 * MIB, transcendentals=0),
        name="write",
    )(inner_final, outer_final)
    late, new_state = lax.optimization_barrier((here, new_state))
    other = lax.ppermute(late, "blk", mates)
    pieces = [before, here, after]
    pieces += [lax.ppermute(before, "blk", mates), other, lax.ppermute(after, "blk", mates)]

    coupled = pl.pallas_call(
        regrid_kernel,
        grid_spec=pltpu.PrefetchScalarGridSpec(
            num_scalar_prefetch=1,
            grid=(1,),
            in_specs=[anywhere] * 6 + [whole],
            out_specs=pl.BlockSpec((fields * rows, columns), lambda i, p: (0, 0)),
            scratch_shapes=[
                VMEM((6 * tiles, fields, TC), BF16),
                VMEM((per_row, fields * rows, TC), F32),
                pltpu.SemaphoreType.DMA((6,)),
            ],
        ),
        out_shape=jax.ShapeDtypeStruct((fields * rows, columns), BF16),
        compiler_params=pltpu.CompilerParams(vmem_limit_bytes=8 * MIB),
        cost_estimate=pl.CostEstimate(flops=10**9, bytes_accessed=16 * MIB, transcendentals=0),
        name="regrid",
    )(positions, *pieces, weights)

    return (
        new_state.reshape(1, levels, rows, columns),
        coupled.reshape(1, fields, rows, columns),
    )


def solution(mesh):
    in_specs = (
        P("sec", None, "blk", None),
        P("sec", None, "blk", None),
        P("sec", None, None),
        P("sec", None),
        P("sec", None, None),
        P("sec", None, None),
        P("blk", None),
        P("sec", "blk", None),
        P("sec", "blk", None, None, None),
    )
    out_specs = (P("sec", None, "blk", None), P("sec", None, "blk", None))
    return jax.shard_map(
        on_device, mesh=mesh, in_specs=in_specs, out_specs=out_specs, check_vma=False
    )
```
